32 devices in a mesh: latent: 4 (over z), row: 2 (over x), col: 4 (over y, core).
Axes of the slice: x: 2, y: 2, z: 4, core: 2. Of those that a mesh axis runs over, the one named last changes fastest.
Arguments:
- observations: bfloat16 [128, 64, 2048], P('col', 'latent', 'row'), may hold values from -6 to 6
- rotation: float32 [64, 4], replicated, may hold values from -0.75 to 0.75
- ordering: int32 [2048], P('row'), may hold values from 0 to 2047, as said below
- working: bfloat16 [4, 2048, 2048], P('latent', 'row', 'col'), as said below
- factor_inverse: bfloat16 [4, 2, 512, 512], P('latent'), as said below
- panel_index: int32 [2], replicated, may hold values from 0 to 3
Outputs:
- trailing: float32 [4, 2048, 2048], P('latent', 'row', 'col')
- panels: bfloat16 [4, 2, 2048, 512], P('latent', None, 'row', 'col')
- whitened: float32 [4, 128, 2048], P('latent', 'col', 'row')
The draws below stay inside these ranges and needn't reach their ends.
Inputs may be any that keep to these rules, and one draw needn't show every extreme that they name: `ordering`: a permutation of the stations that maps each block of 1024 consecutive positions onto the same block. `working`: symmetric in its last two dimensions. `factor_inverse`: lower triangular in its last two dimensions, with a positive diagonal.
All inputs are finite; a program needn't handle non-finite values.
Results may differ from the reference program's by a relative error of at most 0.0047.
Values may be sent and summed in bfloat16 or wider, within the bound.
No kernel may reach another device: no remote copies, remote signals or barrier semaphores. Data moves between devices by JAX's collectives and lax.ppermute only.
A program may use at most 64 MiB of HBM per device.

```python
import jax
import jax.numpy as jnp
from jax import lax

VARS = 64
NB = 512
PANELS = 2
STATIONS = 2048
LATENTS = 4
TIMES = 128
N_ROW = 2


def draw_ordering(key, part):
    block = STATIONS // N_ROW
    keys = jax.random.split(key, N_ROW)
    shuffled = jax.vmap(lambda single: jax.random.permutation(single, block))(keys)
    offsets = (jnp.arange(N_ROW, dtype=jnp.int32) * block)[:, None]
    return (shuffled.astype(jnp.int32) + offsets).reshape(STATIONS)


def draw_working(key, part):

    def one_latent(index):
        single = jax.random.fold_in(jax.random.fold_in(key, 71), index)
        raw = jax.random.normal(jax.random.fold_in(single, 1), (STATIONS, STATIONS), jnp.float32)
        symmetric = 0.5 * (raw + raw.T)
        diag_add = jax.random.uniform(jax.random.fold_in(single, 2), (STATIONS,), jnp.float32, 1.0, 3.0)
        places = jnp.arange(STATIONS)
        symmetric = symmetric + jnp.where(places[:, None] == places[None, :], diag_add[None, :], 0.0)
        return symmetric.astype(jnp.bfloat16)
    return lax.map(one_latent, jnp.arange(LATENTS))


def draw_factor_inverse(key, part):
    shape = (LATENTS, PANELS, NB, NB)
    diag_vals = jax.random.uniform(jax.random.fold_in(key, 11), shape, jnp.float32, 0.06, 0.18)
    lower_vals = jax.random.normal(jax.random.fold_in(key, 12), shape, jnp.float32) * (0.1 / NB ** 0.5)
    rows_at = jnp.arange(NB)[:, None]
    cols_at = jnp.arange(NB)[None, :]
    result = jnp.where(rows_at == cols_at, diag_vals, jnp.where(cols_at < rows_at, lower_vals, 0.0))
    return result.astype(jnp.bfloat16)


def shard_levels(rng, shape, cuts, least, top_value):
    loudness = 1.0
    for dim, blocks in cuts:
        steps = jax.random.uniform(jax.random.fold_in(jax.random.fold_in(rng, 6), dim), (blocks,), jnp.float32, least / len(cuts), top_value / len(cuts))
        loudness = loudness * jnp.repeat(jnp.exp(steps), shape[dim] // blocks).reshape((-1,) + (1,) * (len(shape) - 1 - dim))
    return loudness


def bell_draw(own_key, extent, scale, limit, pieces=(), kind=jnp.bfloat16):
    loudness = shard_levels(own_key, extent, pieces, -0.22, 0.18) if pieces else 1.0
    values = jax.random.normal(own_key, extent, jnp.float32) * scale * loudness
    return jnp.minimum(jnp.maximum(values, -limit), limit).astype(kind)


def setup_inputs(seed: int = 0) -> dict:
    splits = jax.random.split(jax.random.key(seed), 7)
    return {
        "observations": bell_draw(splits[0], (TIMES, VARS, STATIONS), 1.0, 6.0, ((0, 4), (1, 4), (2, 2))),
        "rotation": bell_draw(splits[1], (VARS, LATENTS), VARS ** -0.5, 0.75, (), jnp.float32),
        "ordering": draw_ordering(jax.random.fold_in(splits[6], 71), 0),
        "working": draw_working(jax.random.fold_in(splits[6], 71), 0),
        "factor_inverse": draw_factor_inverse(jax.random.fold_in(splits[6], 71), 0),
        "panel_index": jax.random.randint(splits[5], (PANELS,), 0, STATIONS // NB).astype(jnp.int32),
    }


def reference(observations, rotation, ordering, working, factor_inverse, panel_index):
    rotated = jnp.einsum("tvs,vl->lts", observations.astype(jnp.float32), rotation, precision=lax.Precision.HIGHEST)
    fields = jnp.take(rotated, ordering, axis=2)

    def one_latent(packed):
        tile, inverses, field = packed
        matrix = tile.astype(jnp.float32)
        factors = []
        for panel in range(PANELS):
            inverse = inverses[panel].astype(jnp.float32)
            start = (panel_index[panel] * NB).astype(jnp.int32)
            column_block = lax.dynamic_slice_in_dim(matrix, start, NB, 1).astype(jnp.bfloat16).astype(jnp.float32)
            factor = jnp.dot(column_block, inverse.T, precision=lax.Precision.HIGHEST).astype(jnp.bfloat16)
            rhs_part = lax.dynamic_slice_in_dim(field, start, NB, 1)
            solved = jnp.dot(rhs_part, inverse.T, precision=lax.Precision.HIGHEST).astype(jnp.bfloat16)
            wide_factor = factor.astype(jnp.float32)
            matrix = matrix - jnp.dot(wide_factor, wide_factor.T, precision=lax.Precision.HIGHEST)
            field = field - jnp.dot(solved.astype(jnp.float32), wide_factor.T, precision=lax.Precision.HIGHEST)
            factors.append(factor)
        return matrix, jnp.stack(factors), field

    trailing, panels, whitened = lax.map(one_latent, (working, factor_inverse, fields))
    return (trailing, panels, whitened)
```

```python
import functools

import jax
import jax.numpy as jnp
from jax import lax
from jax.experimental import pallas as pl
from jax.experimental.pallas import tpu as pltpu
from jax.sharding import PartitionSpec as P

F32 = jnp.float32
BF16 = jnp.bfloat16
VMEM = pl.BlockSpec(memory_space=pltpu.VMEM)
SMEM = pl.BlockSpec(memory_space=pltpu.SMEM)
PARAMS = pltpu.CompilerParams(vmem_limit_bytes=48 * 1024 * 1024)


def dot(a, b, ca, cb):
    return lax.dot_general(a, b, (((ca,), (cb,)), ((), ())), preferred_element_type=F32)


def pieces(x, count):
    out = []
    for _ in range(count):
        piece = x.astype(BF16)
        out.append(piece)
        x = x - piece.astype(F32)
    return out


def rotate_kernel(place, obs, rotation, order, out):
    times, own_vars, stations = obs.shape
    all_vars, latents = rotation.shape
    flat = obs[...].reshape(times * own_vars, stations)
    shape = (latents * times, times * own_vars)
    left = lax.broadcasted_iota(jnp.int32, shape, 0)
    right = lax.broadcasted_iota(jnp.int32, shape, 1)
    keep = lax.rem(left, times) == lax.div(right, own_vars)
    sel_l = lax.broadcasted_iota(jnp.int32, (latents * times, latents), 0)
    sel_l = lax.div(sel_l, times) == lax.broadcasted_iota(jnp.int32, (latents * times, latents), 1)
    pick_v = lax.broadcasted_iota(jnp.int32, (all_vars, times * own_vars), 1)
    pick_v = lax.rem(pick_v, own_vars) + place[0] * own_vars
    pick_v = pick_v == lax.broadcasted_iota(jnp.int32, (all_vars, times * own_vars), 0)
    sel_l = sel_l.astype(F32).astype(BF16)
    pick_v = pick_v.astype(F32).astype(BF16)
    total = None
    for piece in pieces(rotation[...], 3):
        wide = dot(sel_l, piece, 1, 1).astype(BF16)
        wide = dot(wide, pick_v, 1, 0)
        wide = jnp.where(keep, wide, 0.0).astype(BF16)
        part = dot(wide, flat, 1, 0)
        total = part if total is None else total + part
    local = order[...] - place[1] * stations
    spread = lax.broadcasted_iota(jnp.int32, (stations, stations), 0) == local
    spread = spread.astype(F32).astype(BF16)
    moved = dot(total.astype(BF16), spread, 1, 0)
    out[...] = moved.astype(BF16).reshape(out.shape)


def factor_kernel(
    place, index, working, sibling, x_own, x_sib, y_own, y_sib, relay, inverse, field, rhs_far,
    trailing, panels, whitened, rows0, rows1, cols0, cols1, cross, block, rhs_near,
):
    row, col = place[0], place[1]
    tall, width = working.shape
    share = panels.shape[2]
    half = tall // width
    mine = lax.rem(col, half)
    col_half = lax.div(col, half)
    panel0, panel1 = index[0], index[1]
    half0, half1 = lax.div(panel0, half), lax.div(panel1, half)

    def within(panel):
        return pl.ds(pl.multiple_of(lax.rem(panel, half) * width, width), width)

    def received(panel):
        return within(panel) if x_own.shape[0] == tall else pl.ds(0, width)

    def part(number):
        return pl.ds(pl.multiple_of(number * width, width), width)

    inv0, inv1 = inverse[0], inverse[1]

    def rows_by_columns(panel, panel_half, body):
        @pl.when((col_half == panel_half) & (panel == col))
        def _():
            body(working)

        @pl.when((col_half == panel_half) & (panel != col))
        def _():
            body(sibling)

    def rows_by_rows(panel, panel_half, body):
        @pl.when((col_half != panel_half) & (row == panel_half))
        def _():
            body(y_own.at[received(panel)], part(mine))
            body(y_sib.at[received(panel)], part(half - 1 - mine))

        @pl.when((col_half != panel_half) & (row != panel_half))
        def _():
            body(x_own.at[received(panel)], part(mine))
            body(x_sib.at[received(panel)], part(half - 1 - mine))

    def own_columns(panel, panel_half):
        @pl.when(row == panel_half)
        def _():
            block[...] = working[within(panel)]

        @pl.when(row != panel_half)
        def _():
            block[...] = x_own[received(panel)]

    own_columns(panel0, half0)
    cols0[...] = dot(inv0, block[...], 1, 0).astype(BF16)

    def straight0(ref):
        rows0[...] = dot(ref[...], inv0, 1, 1).astype(BF16)

    def turned0(ref, where):
        rows0[where] = dot(ref[...], inv0, 0, 1).astype(BF16)

    rows_by_columns(panel0, half0, straight0)
    rows_by_rows(panel0, half0, turned0)

    @pl.when(row == half1)
    def _():
        cross[...] = rows0[within(panel1)]

    @pl.when((row != half1) & (row == half0) & (col_half == half1) & (col == panel1))
    def _():
        cross[...] = dot(working[within(panel0)], inv0, 0, 1).astype(BF16)

    @pl.when((row != half1) & (row == half0) & (col_half == half1) & (col != panel1))
    def _():
        cross[...] = dot(sibling[within(panel0)], inv0, 0, 1).astype(BF16)

    @pl.when((row != half1) & (row == half0) & (col_half != half1) & (col == panel0))
    def _():
        cross[...] = dot(x_own[received(panel1)], inv0, 1, 1).astype(BF16)

    @pl.when((row != half1) & (row == half0) & (col_half != half1) & (col != panel0))
    def _():
        cross[...] = dot(x_sib[received(panel1)], inv0, 1, 1).astype(BF16)

    @pl.when((row != half1) & (row != half0) & (col_half == half1) & (col == panel1))
    def _():
        cross[...] = cols0[...].astype(F32).T.astype(BF16)

    @pl.when((row != half1) & (row != half0) & (col_half == half1) & (col != panel1))
    def _():
        cross[...] = dot(x_sib[received(panel0)], inv0, 0, 1).astype(BF16)

    @pl.when((row != half1) & (row != half0) & (col_half != half1))
    def _():
        cross[...] = dot(relay[...], inv0, 0, 1).astype(BF16)

    own_columns(panel1, half1)
    updated = block[...].astype(F32) - dot(cross[...], cols0[...], 1, 0)
    cols1[...] = dot(inv1, updated.astype(BF16), 1, 0).astype(BF16)

    def straight1(ref):
        later = ref[...].astype(F32) - dot(rows0[...], cross[...], 1, 1)
        rows1[...] = dot(later.astype(BF16), inv1, 1, 1).astype(BF16)

    def turned1(ref, where):
        later = ref[...].astype(F32) - dot(cross[...], rows0[where], 1, 1)
        rows1[where] = dot(later.astype(BF16), inv1, 0, 1).astype(BF16)

    rows_by_columns(panel1, half1, straight1)
    rows_by_rows(panel1, half1, turned1)

    trailing[...] = (
        working[...].astype(F32)
        - dot(rows0[...], cols0[...], 1, 0)
        - dot(rows1[...], cols1[...], 1, 0)
    )
    lanes = pl.ds(pl.multiple_of(col * share, share), share)
    panels[0] = rows0[:, lanes]
    panels[1] = rows1[:, lanes]

    def near(number, panel, panel_half):
        @pl.when(row == panel_half)
        def _():
            rhs_near[number] = field[:, within(panel)]

        @pl.when(row != panel_half)
        def _():
            rhs_near[number] = rhs_far[number].astype(F32)

    near(0, panel0, half0)
    near(1, panel1, half1)

    def solve(rhs, inv):
        return sum(dot(piece, inv, 1, 1) for piece in pieces(rhs, 2)).astype(BF16)

    solved0 = solve(rhs_near[0], inv0)
    solved1 = solve(rhs_near[1] - dot(solved0, cross[...], 1, 1), inv1)
    whitened[...] = field[...] - dot(solved0, rows0[...], 1, 1) - dot(solved1, rows1[...], 1, 1)


def local(observations, rotation, ordering, working, factor_inverse, panel_index):
    latents = rotation.shape[1]
    latent_count = lax.axis_size("latent")
    times, own_vars, stations = observations.shape
    matrix = working[0]
    inverse = factor_inverse[0]
    tall, wide = matrix.shape
    panel_count, width, _ = inverse.shape
    half = tall // width
    share = width // lax.axis_size("col")
    row, col, latent = lax.axis_index("row"), lax.axis_index("col"), lax.axis_index("latent")

    def across_rows(x):
        return lax.ppermute(x, "row", [(0, 1), (1, 0)])

    def across_cols(x, bit):
        return lax.ppermute(x, "col", [(i, i ^ bit) for i in range(lax.axis_size("col"))])

    half0, half1 = panel_index[0] // half, panel_index[1] // half
    same_half = half0 == half1
    same_panel = panel_index[0] == panel_index[1]

    def make_field():
        terms = pl.pallas_call(
            rotate_kernel,
            out_shape=jax.ShapeDtypeStruct((latents, times, stations), BF16),
            in_specs=[SMEM, VMEM, VMEM, VMEM],
            out_specs=VMEM,
            compiler_params=PARAMS,
        )(jnp.stack([latent, row]), observations, rotation, ordering[None])
        own = lax.dynamic_index_in_dim(terms, latent, 0, keepdims=False).astype(F32)
        for shift in range(1, latent_count):
            target = lax.rem(latent + shift, latent_count)
            sent = lax.dynamic_index_in_dim(terms, target, 0, keepdims=False)
            pairs = [(i, (i + shift) % latent_count) for i in range(latent_count)]
            own = own + lax.ppermute(sent, "latent", pairs).astype(F32)
        rhs = jnp.stack(
            [
                lax.dynamic_slice_in_dim(own, (panel_index[p] % half) * width, width, 1)
                for p in range(panel_count)
            ]
        ).astype(BF16)
        return own, across_rows(rhs)

    def finish(x_own, x_sib, y_own, y_sib, relay, sibling, field, rhs_far):
        return pl.pallas_call(
            factor_kernel,
            out_shape=(
                jax.ShapeDtypeStruct((tall, wide), F32),
                jax.ShapeDtypeStruct((panel_count, tall, share), BF16),
                jax.ShapeDtypeStruct((times, stations), F32),
            ),
            in_specs=[SMEM, SMEM] + [VMEM] * 10,
            out_specs=(VMEM, VMEM, VMEM),
            scratch_shapes=[
                pltpu.VMEM((tall, width), BF16),
                pltpu.VMEM((tall, width), BF16),
                pltpu.VMEM((width, wide), BF16),
                pltpu.VMEM((width, wide), BF16),
                pltpu.VMEM((width, width), BF16),
                pltpu.VMEM((width, wide), BF16),
                pltpu.VMEM((panel_count, times, width), F32),
            ],
            compiler_params=PARAMS,
        )(
            jnp.stack([row, col]), panel_index, matrix, sibling, x_own, x_sib, y_own, y_sib, relay,
            inverse, field, rhs_far,
        )

    def run(sent, with_relay):
        x_own = across_rows(sent)
        y_own = across_cols(sent, 2)
        sibling = across_cols(matrix, 1)
        field, rhs_far = make_field()
        x_sib = across_cols(x_own, 1)
        y_sib = across_cols(y_own, 1)
        if with_relay:
            start = 0 if sent.shape[0] == width else (panel_index[0] % half) * width
            first = lax.dynamic_slice_in_dim(x_own, start, width // 2, 0)
            second = lax.dynamic_slice_in_dim(y_own, start + width // 2, width // 2, 0)
            first = across_cols(first, 2)
            second = across_rows(second)
            relay = jnp.concatenate([first, second], 0)
            other = across_cols(relay, 1)
            relay = jnp.where(panel_index[1] % half == col % half, relay, other)
        else:
            relay = x_own
        return finish(x_own, x_sib, y_own, y_sib, relay, sibling, field, rhs_far)

    def cut(panel):
        return lax.dynamic_slice_in_dim(matrix, (panel % half) * width, width, 0)

    def apart():
        return run(cut(jnp.where(half0 == row, panel_index[0], panel_index[1])), False)

    def equal():
        return run(cut(panel_index[0]), True)

    def together():
        return run(matrix, True)

    case = jnp.where(same_panel, 1, jnp.where(same_half, 2, 0))
    trailing, panels, whitened = lax.switch(case, [apart, equal, together])
    return trailing[None], panels[None], whitened[None]


def solution(mesh):
    return jax.shard_map(
        local,
        mesh=mesh,
        in_specs=(
            P("col", "latent", "row"),
            P(),
            P("row"),
            P("latent", "row", "col"),
            P("latent", None, None, None),
            P(),
        ),
        out_specs=(
            P("latent", "row", "col"),
            P("latent", None, "row", "col"),
            P("latent", "col", "row"),
        ),
        check_vma=False,
    )
```

```python
import jax
import jax.numpy as jnp
from jax import lax
from jax.experimental import pallas as pl
from jax.experimental.pallas import tpu as pltpu
from jax.sharding import PartitionSpec as P

F32 = jnp.float32
BF16 = jnp.bfloat16
VMEM = pl.BlockSpec(memory_space=pltpu.VMEM)
SMEM = pl.BlockSpec(memory_space=pltpu.SMEM)
ANY = pl.BlockSpec(memory_space=pl.ANY)
PARAMS = pltpu.CompilerParams(vmem_limit_bytes=48 * 1024 * 1024)

OWN, SIB, ROW_OWN, ROW_SIB, COL_OWN, COL_SIB, POOL = 0, 8, 16, 21, 26, 31, 36


def dot(a, b, ca, cb):
    return lax.dot_general(a, b, (((ca,), (cb,)), ((), ())), preferred_element_type=F32)


def pieces(x, count):
    out = []
    for _ in range(count):
        piece = x.astype(BF16)
        out.append(piece)
        x = x - piece.astype(F32)
    return out


def where(cond, a, b):
    return jnp.where(cond, a, b)


class Place:
    def __init__(self, place, index):
        self.row, self.col = place[0], place[1]
        self.k, self.y = lax.rem(self.col, 2), lax.div(self.col, 2)
        self.q = [index[0], index[1]]
        self.half = [lax.div(q, 2) for q in self.q]
        self.low = [lax.rem(q, 2) for q in self.q]
        self.equal = self.q[0] == self.q[1]
        self.apart = self.half[0] != self.half[1]
        self.together = jnp.logical_not(self.equal | self.apart)
        self.in_row = [self.row == h for h in self.half]
        self.in_col = [self.y == h for h in self.half]
        self.kept = where(self.low[0] == self.k, 0, 1)

    def tile(self, panel_low, a, s):
        return 2 * (2 * panel_low + a) + s

    def sends(self, over_row, n):
        low = where(self.apart & (self.half[0] != self.row), self.low[1], self.low[0])
        s, a = (n // 2 if over_row else 1 - n // 2), n % 2
        plain = self.tile(low, a, s) if n < 4 else 0
        mine = where(self.kept == 0, self.low[0], self.low[1])
        other = where(self.kept == 0, self.low[1], self.low[0])
        first = self.kept == 0
        source = [
            where(first, self.tile(other, 0, 0), self.tile(other, 0, 1)),
            where(first, self.tile(other, 0, 1), self.tile(other, 1, 1)),
            self.tile(mine, 0, 0),
            self.tile(mine, 1, 1),
            self.tile(mine, 1, 0),
        ][n]
        if n == 4:
            return source
        if over_row:
            passed = self.tile(other, n % 2, n // 2)
        else:
            passed = 2 * (2 * self.k + n // 2) + n % 2
        both = where(self.in_row[0] & self.in_col[0], source, passed)
        return where(self.together, both, plain)

    def message(self, over_row, k):
        own, sib = (ROW_OWN, ROW_SIB) if over_row else (COL_OWN, COL_SIB)
        return where(k == self.k, own, sib)

    def diagonal(self, over_row, p, i, j):
        base = self.message(over_row, self.low[p])
        return base + (2 + i if i == j else 4), jnp.int32(1 if (i, j) == (0, 1) else 0)

    def mixed(self, over_row, i, j):
        return self.message(over_row, self.low[i]) + j, jnp.int32(i)

    def pick(self, cond, a, b):
        return where(cond, a[0], b[0]), where(cond, a[1], b[1])

    def rows(self, p, t, s, a):
        here = where(self.q[p] == self.col, OWN, SIB) + 2 * (2 * t + s) + a, jnp.int32(0)
        plain = self.message(False, jnp.int32(t)) + (a if s == 1 else 2 + a), jnp.int32(1)
        same = self.diagonal(False, p, s, a)
        if p == 0:
            cross = self.mixed(False, s, a)
        else:
            cross = self.mixed(False, a, s)
            cross = cross[0], 1 - cross[1]
        both = self.pick(self.low[p] == t, same, cross)
        beside = self.pick(self.together, both, plain)
        passed = self.message(True, jnp.int32(t)) + 2 * s + a, jnp.int32(1)
        kept = self.message(False, jnp.int32(t)) + 2 * s + a, jnp.int32(0)
        far = self.pick(self.together & (self.low[p] == t), kept, passed)
        return self.pick(self.in_col[p], here, self.pick(self.in_row[p], beside, far))

    def cols(self, p, a, s):
        here = self.tile(self.low[p], a, s), jnp.int32(0)
        plain = jnp.int32(ROW_OWN + 2 * s + a), jnp.int32(0)
        kept = jnp.int32(COL_OWN + 2 * s + a), jnp.int32(1)
        passed = self.pick(self.low[p] == self.k, kept, plain)
        same = self.diagonal(True, p, a, s)
        if p == 0:
            cross = self.mixed(True, s, a)
            cross = cross[0], 1 - cross[1]
        else:
            cross = self.mixed(True, a, s)
        source = self.pick(self.low[p] == self.k, same, cross)
        both = self.pick(self.in_col[p], source, passed)
        far = self.pick(self.together, both, plain)
        return self.pick(self.in_row[p], here, far)

    def cross(self, i, a):
        mine = self.pick(self.low[1] == 0, self.rows(0, 0, i, a), self.rows(0, 1, i, a))
        turned = self.pick(self.low[0] == 0, self.rows(1, 0, a, i), self.rows(1, 1, a, i))
        turned = turned[0], 1 - turned[1]
        equal_near = self.message(True, self.low[1]) + 2 * i + a, jnp.int32(1)
        near = self.pick(self.equal, equal_near, self.mixed(True, i, a))
        holder = self.low[0] if a == 0 else 1 - self.low[0]
        equal_far = self.message(i == 1, holder) + 4, jnp.int32(1)
        both_far = self.message(a == 1, self.low[i]) + 4, jnp.int32(i)
        far = self.pick(self.equal, equal_far, both_far)
        outside = self.pick(self.in_col[1], near, far)
        return self.pick(self.in_row[1], mine, self.pick(self.in_row[0], turned, outside))


def quarter_of(ref, number, size):
    down = pl.multiple_of(lax.div(number, 2) * size, size)
    along = pl.multiple_of(lax.rem(number, 2) * size, size)
    return ref.at[pl.ds(down, size), pl.ds(along, size)]


def first_kernel(place, index, working, row1, row2, col1, col2, sems):
    here = Place(place, index)
    size = row1.shape[1]
    copies = []
    for over_row, refs in ((True, (row1, row2)), (False, (col1, col2))):
        for n in range(4):
            copies.append(
                pltpu.make_async_copy(
                    quarter_of(working, here.sends(over_row, n), size),
                    refs[n // 2].at[n % 2],
                    sems.at[len(copies)],
                )
            )
    for copy in copies:
        copy.start()
    for copy in copies:
        copy.wait()


def second_kernel(place, index, working, row_own, row_sib, col_own, col_sib, row_out, col_out, sems):
    here = Place(place, index)
    size = row_out.shape[1]
    source = here.in_row[0] & here.in_col[0]
    own = here.low[0] == here.k
    for n, (got, got_sib, out, which) in enumerate(
        ((col_own, col_sib, row_out, 1), (row_own, row_sib, col_out, 0))
    ):
        sem = sems.at[n]

        @pl.when(source)
        def _():
            pltpu.make_async_copy(
                quarter_of(working, here.sends(True, 4), size), out.at[0], sem
            ).start()

        @pl.when(jnp.logical_not(source) & here.together)
        def _():
            pltpu.make_async_copy(got.at[which], out.at[0], sem).start()

        @pl.when(jnp.logical_not(source) & jnp.logical_not(here.together) & own)
        def _():
            pltpu.make_async_copy(got.at[0], out.at[0], sem).start()

        @pl.when(jnp.logical_not(source | here.together | own))
        def _():
            pltpu.make_async_copy(got_sib.at[1], out.at[0], sem).start()

    pltpu.make_async_copy(row_own.at[0], row_out.at[0], sems.at[0]).wait()
    pltpu.make_async_copy(col_own.at[0], col_out.at[0], sems.at[1]).wait()


def rotate_kernel(place, obs, rotation, order, out):
    times, own_vars, stations = obs.shape
    all_vars, latents = rotation.shape
    flat = obs[...].reshape(times * own_vars, stations)
    shape = (latents * times, times * own_vars)
    left = lax.broadcasted_iota(jnp.int32, shape, 0)
    right = lax.broadcasted_iota(jnp.int32, shape, 1)
    keep = lax.rem(left, times) == lax.div(right, own_vars)
    sel_l = lax.broadcasted_iota(jnp.int32, (latents * times, latents), 0)
    sel_l = lax.div(sel_l, times) == lax.broadcasted_iota(jnp.int32, (latents * times, latents), 1)
    pick_v = lax.broadcasted_iota(jnp.int32, (all_vars, times * own_vars), 1)
    pick_v = lax.rem(pick_v, own_vars) + place[2] * own_vars
    pick_v = pick_v == lax.broadcasted_iota(jnp.int32, (all_vars, times * own_vars), 0)
    sel_l = sel_l.astype(F32).astype(BF16)
    pick_v = pick_v.astype(F32).astype(BF16)
    total = None
    for piece in pieces(rotation[...], 3):
        wide = dot(sel_l, piece, 1, 1).astype(BF16)
        wide = dot(wide, pick_v, 1, 0)
        wide = jnp.where(keep, wide, 0.0).astype(BF16)
        part = dot(wide, flat, 1, 0)
        total = part if total is None else total + part
    local = order[...] - place[0] * stations
    spread = lax.broadcasted_iota(jnp.int32, (stations, stations), 0) == local
    spread = spread.astype(F32).astype(BF16)
    moved = dot(total.astype(BF16), spread, 1, 0)
    out[...] = moved.astype(BF16).reshape(out.shape)


def factor_kernel(
    place, index, working, sibling, row1, row1s, row2, row2s, row3, row3s, col1, col1s, col2, col2s, col3, col3s,
    inverse, field, rhs_far, trailing, panels, whitened,
    pool, blocks, factors0, factors1, turned0, turned1, rhs_near, table, flip, sems,
):
    here = Place(place, index)
    size = pool.shape[1]
    tall, wide = trailing.shape
    width = inverse.shape[1]
    share = panels.shape[2]
    steps = tall // size

    copies = []

    def fetch(source, slot):
        copies.append(pltpu.make_async_copy(source, pool.at[slot], sems.at[slot]))

    for n in range(8):
        fetch(quarter_of(working, jnp.int32(n), size), OWN + n)
        fetch(quarter_of(sibling, jnp.int32(n), size), SIB + n)
    for base, refs in (
        (ROW_OWN, (row1, row2, row3)),
        (ROW_SIB, (row1s, row2s, row3s)),
        (COL_OWN, (col1, col2, col3)),
        (COL_SIB, (col1s, col2s, col3s)),
    ):
        for n in range(5):
            fetch(refs[n // 2].at[n % 2], base + n)
    for copy in copies:
        copy.start()

    entries = []
    for p in range(2):
        entries += [here.rows(p, n // 4, n // 2 % 2, n % 2) for n in range(8)]
    for p in range(2):
        entries += [here.cols(p, n // 2, n % 2) for n in range(4)]
    entries += [here.cross(n // 2, n % 2) for n in range(4)]
    for n, (slot, turn) in enumerate(entries):
        table[n] = slot
        flip[n] = turn
    for copy in copies:
        copy.wait()

    def assemble(n, _):
        for side in range(2):
            slot = table[2 * n + side]
            turn = flip[2 * n + side]
            down = pl.ds(pl.multiple_of(n * size, size), size)
            along = pl.ds(side * size, size)

            @pl.when(turn == 0)
            def _():
                blocks[down, along] = pool[slot]

            @pl.when(turn != 0)
            def _():
                blocks[down, along] = pool[slot].T

        return 0

    lax.fori_loop(0, len(entries) // 2, assemble, 0)

    def strip(n):
        return pl.ds(n * size, size)

    rows0, rows1, cols0, cols1, cross = 0, steps, 2 * steps, 2 * steps + 2, 2 * steps + 4
    inv0, inv1 = inverse[0], inverse[1]

    def factor(n, _):
        n = where(n < steps, n, cross + n - steps)
        to = where(n < steps, n, n - cross + steps)
        got = blocks[pl.ds(pl.multiple_of(n * size, size), size)]
        factors0[pl.ds(pl.multiple_of(to * size, size), size)] = dot(got, inv0, 1, 1).astype(BF16)
        return 0

    lax.fori_loop(0, steps + 2, factor, 0)
    mixed = factors0[pl.ds(tall, width)]
    turned0[...] = dot(inv0, blocks[pl.ds(cols0 * size, width)], 1, 0).astype(BF16)

    def later(n, _):
        down = pl.ds(pl.multiple_of(n * size, size), size)
        got = blocks[pl.ds(pl.multiple_of((n + rows1) * size, size), size)]
        got = got.astype(F32) - dot(factors0[down], mixed, 1, 1)
        factors1[down] = dot(got.astype(BF16), inv1, 1, 1).astype(BF16)
        return 0

    lax.fori_loop(0, steps, later, 0)
    got = blocks[pl.ds(cols1 * size, width)].astype(F32) - dot(mixed, turned0[...], 1, 0)
    turned1[...] = dot(inv1, got.astype(BF16), 1, 0).astype(BF16)

    def update(n, _):
        down = pl.ds(pl.multiple_of(n * size, size), size)
        change = dot(factors0[down], turned0[...], 1, 0) + dot(factors1[down], turned1[...], 1, 0)
        for side in range(2):
            along = pl.ds(side * size, size)
            trailing[down, along] = pool[2 * n + side].astype(F32) - change[:, side * size : (side + 1) * size]
        return 0

    lax.fori_loop(0, steps, update, 0)
    lanes = pl.ds(pl.multiple_of(here.col * share, share), share)
    panels[0] = factors0[pl.ds(0, tall), lanes]
    panels[1] = factors1[:, lanes]

    for p in range(2):
        inside = pl.ds(pl.multiple_of(here.low[p] * width, width), width)

        @pl.when(here.in_row[p])
        def _():
            rhs_near[p] = field[:, inside]

        @pl.when(jnp.logical_not(here.in_row[p]))
        def _():
            rhs_near[p] = rhs_far[p].astype(F32)

    def solve(rhs, inv):
        return sum(dot(piece, inv, 1, 1) for piece in pieces(rhs, 2)).astype(BF16)

    solved0 = solve(rhs_near[0], inv0)
    solved1 = solve(rhs_near[1] - dot(solved0, mixed, 1, 1), inv1)
    whitened[...] = (
        field[...] - dot(solved0, factors0[pl.ds(0, tall)], 1, 1) - dot(solved1, factors1[...], 1, 1)
    )


def local(observations, rotation, ordering, working, factor_inverse, panel_index):
    latents = rotation.shape[1]
    latent_count = lax.axis_size("latent")
    times, own_vars, stations = observations.shape
    matrix = working[0]
    inverse = factor_inverse[0]
    tall, wide = matrix.shape
    panel_count, width, _ = inverse.shape
    size = width // 2
    share = width // lax.axis_size("col")
    row, col, latent = lax.axis_index("row"), lax.axis_index("col"), lax.axis_index("latent")
    place = jnp.stack([row, col, latent])

    def across_rows(x):
        return lax.ppermute(x, "row", [(0, 1), (1, 0)])

    def across_cols(x):
        return lax.ppermute(x, "col", [(i, i ^ 2) for i in range(lax.axis_size("col"))])

    def siblings(x):
        return lax.ppermute(x, "col", [(i, i ^ 1) for i in range(lax.axis_size("col"))])

    pair = jax.ShapeDtypeStruct((2, size, size), BF16)
    one = jax.ShapeDtypeStruct((1, size, size), BF16)
    row1, row2, col1, col2 = pl.pallas_call(
        first_kernel,
        out_shape=(pair,) * 4,
        in_specs=[SMEM, SMEM, ANY],
        out_specs=(ANY,) * 4,
        scratch_shapes=[pltpu.SemaphoreType.DMA((8,))],
        compiler_params=PARAMS,
    )(place, panel_index, matrix)
    row1, col1 = across_rows(row1), across_cols(col1)
    row2, col2 = across_rows(row2), across_cols(col2)
    sibling = siblings(matrix)

    terms = pl.pallas_call(
        rotate_kernel,
        out_shape=jax.ShapeDtypeStruct((latents, times, stations), BF16),
        in_specs=[SMEM, VMEM, VMEM, VMEM],
        out_specs=VMEM,
        compiler_params=PARAMS,
    )(place, observations, rotation, ordering[None])

    row1s, col1s = siblings(row1), siblings(col1)
    row3, col3 = pl.pallas_call(
        second_kernel,
        out_shape=(one,) * 2,
        in_specs=[SMEM, SMEM] + [ANY] * 5,
        out_specs=(ANY,) * 2,
        scratch_shapes=[pltpu.SemaphoreType.DMA((2,))],
        compiler_params=PARAMS,
    )(place, panel_index, matrix, row1, row1s, col1, col1s)
    row3, col3 = across_rows(row3), across_cols(col3)

    field = lax.dynamic_index_in_dim(terms, latent, 0, keepdims=False).astype(F32)
    for shift in range(1, latent_count):
        target = lax.rem(latent + shift, latent_count)
        sent = lax.dynamic_index_in_dim(terms, target, 0, keepdims=False)
        pairs = [(i, (i + shift) % latent_count) for i in range(latent_count)]
        field = field + lax.ppermute(sent, "latent", pairs).astype(F32)
    rhs = jnp.stack(
        [
            lax.dynamic_slice_in_dim(field, (panel_index[p] % 2) * width, width, 1)
            for p in range(panel_count)
        ]
    ).astype(BF16)
    rhs_far = across_rows(rhs)

    row2s, col2s = siblings(row2), siblings(col2)
    row3s, col3s = siblings(row3), siblings(col3)

    trailing, panels, whitened = pl.pallas_call(
        factor_kernel,
        out_shape=(
            jax.ShapeDtypeStruct((tall, wide), F32),
            jax.ShapeDtypeStruct((panel_count, tall, share), BF16),
            jax.ShapeDtypeStruct((times, stations), F32),
        ),
        in_specs=[SMEM, SMEM] + [ANY] * 14 + [VMEM] * 3,
        out_specs=(VMEM, VMEM, VMEM),
        scratch_shapes=[
            pltpu.VMEM((POOL, size, size), BF16),
            pltpu.VMEM((14 * size, width), BF16),
            pltpu.VMEM((tall + width, width), BF16),
            pltpu.VMEM((tall, width), BF16),
            pltpu.VMEM((width, wide), BF16),
            pltpu.VMEM((width, wide), BF16),
            pltpu.VMEM((panel_count, times, width), F32),
            pltpu.SMEM((28,), jnp.int32),
            pltpu.SMEM((28,), jnp.int32),
            pltpu.SemaphoreType.DMA((POOL,)),
        ],
        compiler_params=PARAMS,
    )(
        place, panel_index, matrix, sibling, row1, row1s, row2, row2s, row3, row3s,
        col1, col1s, col2, col2s, col3, col3s, inverse, field, rhs_far,
    )
    return trailing[None], panels[None], whitened[None]


def solution(mesh):
    return jax.shard_map(
        local,
        mesh=mesh,
        in_specs=(
            P("col", "latent", "row"),
            P(),
            P("row"),
            P("latent", "row", "col"),
            P("latent", None, None, None),
            P(),
        ),
        out_specs=(
            P("latent", "row", "col"),
            P("latent", None, "row", "col"),
            P("latent", "col", "row"),
        ),
        check_vma=False,
    )
```

```python
import jax
import jax.numpy as jnp
from jax import lax
from jax.experimental import pallas as pl
from jax.experimental.pallas import tpu as pltpu
from jax.sharding import PartitionSpec as P

F32 = jnp.float32
BF16 = jnp.bfloat16
VMEM = pl.BlockSpec(memory_space=pltpu.VMEM)
SMEM = pl.BlockSpec(memory_space=pltpu.SMEM)
ANY = pl.BlockSpec(memory_space=pl.ANY)
HBM = pl.BlockSpec(memory_space=pltpu.HBM)
PARAMS = pltpu.CompilerParams(vmem_limit_bytes=24 * 1024 * 1024)
WIDE = pltpu.CompilerParams(vmem_limit_bytes=60 * 1024 * 1024)

OWN, SIB, FIRST, FIRST_SIB, SECOND, SECOND_SIB, THIRD, THIRD_SIB, POOL = 0, 8, 16, 20, 24, 28, 32, 35, 38


def dot(a, b, ca, cb):
    return lax.dot_general(a, b, (((ca,), (cb,)), ((), ())), preferred_element_type=F32)


def pieces(x, count):
    out = []
    for _ in range(count):
        piece = x.astype(BF16)
        out.append(piece)
        x = x - piece.astype(F32)
    return out


def where(cond, a, b):
    return jnp.where(cond, a, b)


class Place:
    def __init__(self, index):
        self.row, self.col = lax.axis_index("row"), lax.axis_index("col")
        self.k, self.y = lax.rem(self.col, 2), lax.div(self.col, 2)
        self.q = [index[0], index[1]]
        self.half = [lax.div(q, 2) for q in self.q]
        self.low = [lax.rem(q, 2) for q in self.q]
        self.equal = self.q[0] == self.q[1]
        self.apart = self.half[0] != self.half[1]
        self.together = jnp.logical_not(self.equal | self.apart)
        self.in_row = [self.row == h for h in self.half]
        self.in_col = [self.y == h for h in self.half]

    def tile(self, panel_low, a, s):
        return 2 * (2 * panel_low + a) + s

    def sends(self, n):
        k = self.k
        s, a = n // 2, n % 2
        low = where(self.apart & (self.half[0] != self.row), self.low[1], self.low[0])
        first = self.low[0] == k
        source = [
            where(first, self.tile(1 - k, 0, 0), self.tile(1 - k, 0, 1)),
            where(first, self.tile(1 - k, 0, 1), self.tile(1 - k, 1, 1)),
            self.tile(k, 0, 0),
            self.tile(k, 1, 1),
        ][n]
        both = where(self.in_row[0], self.tile(1 - k, a, s), 2 * (2 * k + s) + a)
        both = where(self.in_row[0] & self.in_col[0], source, both)
        return where(self.together, both, self.tile(low, a, s))

    def message(self, over_row, k):
        first = k == 0 if over_row else k != 0
        return where(k == self.k, where(first, FIRST, SECOND), where(first, FIRST_SIB, SECOND_SIB))

    def third(self, k):
        return where(k == self.k, THIRD, THIRD_SIB)

    def diagonal(self, over_row, p, i, j):
        if i == j:
            return self.message(over_row, self.low[p]) + 2 + i, jnp.int32(0)
        return self.third(1 if over_row else 0) + self.low[p], jnp.int32(1 if i == 0 else 0)

    def mixed(self, over_row, i, j):
        return self.message(over_row, self.low[i]) + j, jnp.int32(i)

    def pick(self, cond, a, b):
        return where(cond, a[0], b[0]), where(cond, a[1], b[1])

    def rows(self, p, t, s, a):
        here = where(self.q[p] == self.col, OWN, SIB) + 2 * (2 * t + s) + a, jnp.int32(0)
        plain = self.message(False, jnp.int32(t)) + 2 * s + a, jnp.int32(1)
        same = self.diagonal(False, p, s, a)
        if p == 0:
            cross = self.mixed(False, s, a)
        else:
            cross = self.mixed(False, a, s)
            cross = cross[0], 1 - cross[1]
        both = self.pick(self.low[p] == t, same, cross)
        beside = self.pick(self.together, both, plain)
        passed = self.message(True, jnp.int32(t)) + 2 * s + a, jnp.int32(1)
        kept = self.message(False, jnp.int32(t)) + 2 * s + a, jnp.int32(0)
        far = self.pick(self.together & (self.low[p] == t), kept, passed)
        return self.pick(self.in_col[p], here, self.pick(self.in_row[p], beside, far))

    def cols(self, p, a, s):
        here = self.tile(self.low[p], a, s), jnp.int32(0)
        plain = self.message(True, self.k) + 2 * s + a, jnp.int32(0)
        kept = self.message(False, self.k) + 2 * s + a, jnp.int32(1)
        passed = self.pick(self.low[p] == self.k, kept, plain)
        same = self.diagonal(True, p, a, s)
        if p == 0:
            cross = self.mixed(True, s, a)
            cross = cross[0], 1 - cross[1]
        else:
            cross = self.mixed(True, a, s)
        source = self.pick(self.low[p] == self.k, same, cross)
        both = self.pick(self.in_col[p], source, passed)
        far = self.pick(self.together, both, plain)
        return self.pick(self.in_row[p], here, far)

    def cross(self, i, a):
        mine = self.pick(self.low[1] == 0, self.rows(0, 0, i, a), self.rows(0, 1, i, a))
        turned = self.pick(self.low[0] == 0, self.rows(1, 0, a, i), self.rows(1, 1, a, i))
        turned = turned[0], 1 - turned[1]
        equal_near = self.message(True, self.low[1]) + 2 * i + a, jnp.int32(1)
        near = self.pick(self.equal, equal_near, self.mixed(True, i, a))
        equal_far = self.third(self.low[0]) + i + a, jnp.int32(1 if i < a else 0)
        both_far = self.third(self.low[i]) + a, jnp.int32(i)
        far = self.pick(self.equal, equal_far, both_far)
        outside = self.pick(self.in_col[1], near, far)
        return self.pick(self.in_row[1], mine, self.pick(self.in_row[0], turned, outside))


def quarter_of(tile, number, size):
    down = pl.multiple_of(lax.div(number, 2) * size, size)
    along = pl.multiple_of(lax.rem(number, 2) * size, size)
    return tile[pl.ds(down, size), pl.ds(along, size)]


def first_kernel(index_far, working, sent, index, tile, sems):
    copies = [
        pltpu.make_async_copy(index_far, index, sems.at[0]),
        pltpu.make_async_copy(working, tile, sems.at[1]),
    ]
    for copy in copies:
        copy.start()
    copies[0].wait()
    here = Place(index)
    copies[1].wait()
    for n in range(sent.shape[0]):
        sent[n] = quarter_of(tile, here.sends(n), sent.shape[1])


def third_kernel(index, working, sibling, got, _, sent, token, sems):
    here = Place(index)
    size = sent.shape[1]
    source = here.together & here.in_row[0] & here.in_col[0]
    token[...] = jnp.zeros_like(token)

    def far(tile, k, n):
        number = here.tile(k, 1, 0)
        down = pl.ds(pl.multiple_of(lax.div(number, 2) * size, size), size)
        return pltpu.make_async_copy(tile.at[down, pl.ds(0, size)], sent.at[k], sems.at[n])

    @pl.when(source)
    def _():
        far(working, here.k, 0).start()
        far(sibling, 1 - here.k, 1).start()
        far(working, here.k, 0).wait()
        far(sibling, 1 - here.k, 1).wait()

    @pl.when(jnp.logical_not(source))
    def _():
        sent[0] = got[0]
        sent[1] = got[1]

    sent[2] = got[3]


def tie_kernel(_, __, ___):
    pass


TOKEN = jax.ShapeDtypeStruct((8, 128), F32)


def tie(x, *after, params=PARAMS):
    for other in after:
        x = pl.pallas_call(
            tie_kernel,
            out_shape=jax.ShapeDtypeStruct(x.shape, x.dtype),
            in_specs=[ANY, ANY],
            out_specs=ANY,
            input_output_aliases={0: 0},
            compiler_params=params,
        )(x, other)
    return x


def rotate_kernel(obs_far, rotation_far, order_far, _, token, own, *rest):
    sent, (obs, rotation, order, moved, sems) = rest[:-5], rest[-5:]
    pairs = ((order_far, order), (rotation_far, rotation), (obs_far, obs))
    copies = [pltpu.make_async_copy(far, near, sems.at[n]) for n, (far, near) in enumerate(pairs)]
    for copy in copies:
        copy.start()
    row, latent = lax.axis_index("row"), lax.axis_index("latent")
    times, own_vars, stations = obs.shape
    latents, all_vars = rotation.shape
    token[...] = jnp.zeros_like(token)
    copies[0].wait()
    local = order[...] - row * stations
    spread = lax.broadcasted_iota(jnp.int32, (stations, stations), 0) == local
    spread = spread.astype(F32).astype(BF16)
    copies[1].wait()
    shape = (latents * times, times * own_vars)
    left = lax.broadcasted_iota(jnp.int32, shape, 0)
    right = lax.broadcasted_iota(jnp.int32, shape, 1)
    keep = lax.rem(left, times) == lax.div(right, own_vars)
    sel_l = lax.broadcasted_iota(jnp.int32, (latents * times, latents), 0)
    sel_l = lax.div(sel_l, times) == lax.broadcasted_iota(jnp.int32, (latents * times, latents), 1)
    pick_v = lax.broadcasted_iota(jnp.int32, (all_vars, times * own_vars), 1)
    pick_v = lax.rem(pick_v, own_vars) + latent * own_vars
    pick_v = pick_v == lax.broadcasted_iota(jnp.int32, (all_vars, times * own_vars), 0)
    sel_l = sel_l.astype(F32).astype(BF16)
    pick_v = pick_v.astype(F32).astype(BF16)
    lefts = []
    for piece in pieces(rotation[...], 3):
        wide = dot(sel_l, piece, 1, 0).astype(BF16)
        wide = dot(wide, pick_v, 1, 0)
        lefts.append(jnp.where(keep, wide, 0.0).astype(BF16))
    copies[2].wait()
    flat = obs[...].reshape(times * own_vars, stations)
    total = sum(dot(wide, flat, 1, 0) for wide in lefts)
    moved[...] = dot(total.astype(BF16), spread, 1, 0).reshape(moved.shape)
    own[...] = moved[latent]
    for shift, out in enumerate(sent, 1):
        out[...] = moved[lax.rem(latent + shift, latents)].astype(BF16)


def field_kernel(index, _, own, *rest):
    got, (field, rhs) = rest[:-2], rest[-2:]
    total = own[...]
    for part in got:
        total = total + part[...].astype(F32)
    field[...] = total
    width = rhs.shape[2]
    for p in range(rhs.shape[0]):
        inside = pl.ds(pl.multiple_of(lax.rem(index[p], 2) * width, width), width)
        rhs[p] = field[:, inside].astype(BF16)


def entries_of(here):
    entries = []
    for p in range(2):
        entries += [here.rows(p, n // 4, n // 2 % 2, n % 2) for n in range(8)]
    for p in range(2):
        entries += [here.cols(p, n // 2, n % 2) for n in range(4)]
    return entries + [here.cross(n // 2, n % 2) for n in range(4)]


def is_late(slot):
    return slot >= SECOND


def assemble(blocks, size, table, flip, wanted, load, earlier=None):
    def step(n, _):
        for side in range(2):
            slot = table[2 * n + side]
            turn = flip[2 * n + side]
            down = pl.ds(pl.multiple_of(n * size, size), size)
            along = pl.ds(side * size, size)

            if earlier is not None:

                @pl.when(jnp.logical_not(wanted(slot)))
                def _():
                    blocks[down, along] = earlier[down, along]

            @pl.when(wanted(slot) & (turn == 0))
            def _():
                blocks[down, along] = load(slot)

            @pl.when(wanted(slot) & (turn != 0))
            def _():
                blocks[down, along] = load(slot).T

        return 0

    lax.fori_loop(0, blocks.shape[0] // size, step, 0)


def early_kernel(index, working, sibling, first, first_sib, _, blocks, table, flip, pool):
    here = Place(index)
    size = pool.shape[1]
    for n, (slot, turn) in enumerate(entries_of(here)):
        table[n] = slot
        flip[n] = turn

    def tiles(n, _):
        down = pl.ds(pl.multiple_of(n * size, size), size)
        for side in range(2):
            along = pl.ds(side * size, size)
            pool[OWN + 2 * n + side] = working[down, along]
            pool[SIB + 2 * n + side] = sibling[down, along]
        return 0

    lax.fori_loop(0, working.shape[0] // size, tiles, 0)
    pool[pl.ds(FIRST, 4)] = first[...]
    pool[pl.ds(FIRST_SIB, 4)] = first_sib[...]
    assemble(blocks, size, table, flip, lambda slot: jnp.logical_not(is_late(slot)), lambda slot: pool[slot])


def factor_kernel(
    index, table, flip, working, earlier, second, second_sib, third, third_sib,
    inverse, field, rhs_far, trailing, panels, whitened,
    blocks, pool, factors0, factors1, turned0, turned1, rhs_near, result, sems,
):
    here = Place(index)
    size = pool.shape[1]
    tall, wide = working.shape
    width = inverse.shape[1]
    share = panels.shape[2]

    base = 0
    for ref in (second, second_sib, third, third_sib):
        pool[pl.ds(base, ref.shape[0])] = ref[...]
        base += ref.shape[0]

    def load(slot):
        return pool[slot - SECOND]

    assemble(blocks, size, table, flip, is_late, load, earlier)

    rows0, rows1 = pl.ds(0, tall), pl.ds(tall, tall)
    cols0, cols1 = pl.ds(2 * tall, width), pl.ds(2 * tall + width, width)
    cross = pl.ds(2 * tall + 2 * width, width)
    inv0, inv1 = inverse[0], inverse[1]

    factors0[pl.ds(tall, width)] = dot(blocks[cross], inv0, 1, 1).astype(BF16)
    turned0[...] = dot(inv0, blocks[cols0], 1, 0).astype(BF16)
    factors0[rows0] = dot(blocks[rows0], inv0, 1, 1).astype(BF16)
    mixed = factors0[pl.ds(tall, width)]

    got = blocks[cols1].astype(F32) - dot(mixed, turned0[...], 1, 0)
    turned1[...] = dot(inv1, got.astype(BF16), 1, 0).astype(BF16)
    got = blocks[rows1].astype(F32) - dot(factors0[rows0], mixed, 1, 1)
    factors1[...] = dot(got.astype(BF16), inv1, 1, 1).astype(BF16)

    lanes = pl.ds(pl.multiple_of(here.col * share, share), share)
    copies = [
        pltpu.make_async_copy(factors0.at[rows0, lanes], panels.at[0], sems.at[0]),
        pltpu.make_async_copy(factors1.at[:, lanes], panels.at[1], sems.at[1]),
    ]
    copies[0].start()
    copies[1].start()
    parts = sems.shape[0] - 2
    for n in range(parts):
        down = pl.ds(n * tall // parts, tall // parts)
        change = dot(factors0[down], turned0[...], 1, 0) + dot(factors1[down], turned1[...], 1, 0)
        result[down] = working[down].astype(F32) - change
        copies.append(pltpu.make_async_copy(result.at[down], trailing.at[down], sems.at[2 + n]))
        copies[-1].start()

    for p in range(2):
        inside = pl.ds(pl.multiple_of(here.low[p] * width, width), width)

        @pl.when(here.in_row[p])
        def _():
            rhs_near[p] = field[:, inside]

        @pl.when(jnp.logical_not(here.in_row[p]))
        def _():
            rhs_near[p] = rhs_far[p].astype(F32)

    def solve(rhs, inv):
        return sum(dot(piece, inv, 1, 1) for piece in pieces(rhs, 2)).astype(BF16)

    solved0 = solve(rhs_near[0], inv0)
    solved1 = solve(rhs_near[1] - dot(solved0, mixed, 1, 1), inv1)
    whitened[...] = field[...] - dot(solved0, factors0[rows0], 1, 1) - dot(solved1, factors1[...], 1, 1)
    for copy in copies:
        copy.wait()


def local(observations, rotation, ordering, working, factor_inverse, panel_index):
    latents = rotation.shape[1]
    latent_count = lax.axis_size("latent")
    times, own_vars, stations = observations.shape
    matrix = working[0]
    inverse = factor_inverse[0]
    tall, wide = matrix.shape
    panel_count, width, _ = inverse.shape
    size = width // 2
    share = width // lax.axis_size("col")

    cols = lax.axis_size("col")

    def across_rows(x):
        return lax.ppermute(x, "row", [(0, 1), (1, 0)])

    def siblings(x):
        return lax.ppermute(x, "col", [(i, i ^ 1) for i in range(cols)])

    def neighbours(x, row_first):
        pairs = []
        for i in range(2):
            for j in range(cols):
                over_row = (j % 2 == 0) == row_first
                to = (1 - i, j) if over_row else (i, j ^ 2)
                pairs.append((i * cols + j, to[0] * cols + to[1]))
        return lax.ppermute(x, ("row", "col"), pairs)

    message = jax.ShapeDtypeStruct((4, size, size), BF16)
    extra = jax.ShapeDtypeStruct((3, size, size), BF16)
    sibling = siblings(matrix)
    sent_message = pl.pallas_call(
        first_kernel,
        out_shape=message,
        in_specs=[ANY] * 2,
        out_specs=VMEM,
        scratch_shapes=[
            pltpu.SMEM((2,), jnp.int32),
            pltpu.VMEM(matrix.shape, BF16),
            pltpu.SemaphoreType.DMA((2,)),
        ],
        compiler_params=WIDE,
    )(panel_index, matrix)
    first = neighbours(sent_message, True)

    token, own, *sent = pl.pallas_call(
        rotate_kernel,
        out_shape=[TOKEN, jax.ShapeDtypeStruct((times, stations), F32)]
        + [jax.ShapeDtypeStruct((times, stations), BF16)] * (latent_count - 1),
        in_specs=[ANY] * 4,
        out_specs=[VMEM] * (1 + latent_count),
        scratch_shapes=[
            pltpu.VMEM(observations.shape, BF16),
            pltpu.VMEM(rotation.shape[::-1], F32),
            pltpu.VMEM((1, stations), jnp.int32),
            pltpu.VMEM((latents, times, stations), F32),
            pltpu.SemaphoreType.DMA((3,)),
        ],
        compiler_params=WIDE,
    )(observations, rotation.T, ordering[None], sent_message)
    second = neighbours(tie(sent_message, token, params=WIDE), False)
    got = []
    for shift, part in enumerate(sent, 1):
        pairs = [(i, (i + shift) % latent_count) for i in range(latent_count)]
        got.append(lax.ppermute(part, "latent", pairs))

    first_sib = siblings(first)
    sent_third, third_token = pl.pallas_call(
        third_kernel,
        out_shape=(extra, TOKEN),
        in_specs=[SMEM, ANY, ANY, VMEM, ANY],
        out_specs=(VMEM, VMEM),
        scratch_shapes=[pltpu.SemaphoreType.DMA((2,))],
        compiler_params=PARAMS,
    )(panel_index, matrix, sibling, first, token)
    third = neighbours(sent_third, False)

    field, rhs = pl.pallas_call(
        field_kernel,
        out_shape=(
            jax.ShapeDtypeStruct((times, stations), F32),
            jax.ShapeDtypeStruct((panel_count, times, width), BF16),
        ),
        in_specs=[SMEM, ANY] + [VMEM] * latent_count,
        out_specs=(VMEM, VMEM),
        compiler_params=PARAMS,
    )(panel_index, token, own, *got)
    rhs_far = across_rows(rhs)

    second = tie(second, third_token, rhs)
    second_sib, third_sib = siblings(second), siblings(third)

    block_shape = jax.ShapeDtypeStruct((14 * size, width), BF16)
    table_shape = jax.ShapeDtypeStruct((28,), jnp.int32)
    blocks, table, flip = pl.pallas_call(
        early_kernel,
        out_shape=(block_shape, table_shape, table_shape),
        in_specs=[SMEM] + [VMEM] * 4 + [ANY],
        out_specs=(VMEM, SMEM, SMEM),
        scratch_shapes=[pltpu.VMEM((POOL, size, size), BF16)],
        compiler_params=PARAMS,
    )(panel_index, matrix, sibling, first, first_sib, third_token)

    trailing, panels, whitened = pl.pallas_call(
        factor_kernel,
        out_shape=(
            jax.ShapeDtypeStruct((tall, wide), F32),
            jax.ShapeDtypeStruct((panel_count, tall, share), BF16),
            jax.ShapeDtypeStruct((times, stations), F32),
        ),
        in_specs=[SMEM] * 3 + [VMEM] * 9,
        out_specs=(HBM, HBM, VMEM),
        scratch_shapes=[
            pltpu.VMEM(block_shape.shape, BF16),
            pltpu.VMEM((POOL - SECOND, size, size), BF16),
            pltpu.VMEM((tall + width, width), BF16),
            pltpu.VMEM((tall, width), BF16),
            pltpu.VMEM((width, wide), BF16),
            pltpu.VMEM((width, wide), BF16),
            pltpu.VMEM((panel_count, times, width), F32),
            pltpu.VMEM((tall, wide), F32),
            pltpu.SemaphoreType.DMA((4,)),
        ],
        compiler_params=PARAMS,
    )(
        panel_index, table, flip, matrix, blocks, second, second_sib, third, third_sib,
        inverse, field, rhs_far,
    )
    return trailing[None], panels[None], whitened[None]


def solution(mesh):
    return jax.shard_map(
        local,
        mesh=mesh,
        in_specs=(
            P("col", "latent", "row"),
            P(),
            P("row"),
            P("latent", "row", "col"),
            P("latent", None, None, None),
            P(),
        ),
        out_specs=(
            P("latent", "row", "col"),
            P("latent", None, "row", "col"),
            P("latent", "col", "row"),
        ),
        check_vma=False,
    )
```

```python
import jax
import jax.numpy as jnp
from jax import lax
from jax.experimental import pallas as pl
from jax.experimental.pallas import tpu as pltpu
from jax.sharding import PartitionSpec as P

F32 = jnp.float32
BF16 = jnp.bfloat16
VMEM = pl.BlockSpec(memory_space=pltpu.VMEM)
SMEM = pl.BlockSpec(memory_space=pltpu.SMEM)
ANY = pl.BlockSpec(memory_space=pl.ANY)
HBM = pl.BlockSpec(memory_space=pltpu.HBM)
PARAMS = pltpu.CompilerParams(vmem_limit_bytes=24 * 1024 * 1024)
WIDE = pltpu.CompilerParams(vmem_limit_bytes=60 * 1024 * 1024)

OWN, SIB, FIRST, FIRST_SIB, SECOND, SECOND_SIB, PASSED, PASSED_SIB, POOL = 0, 8, 16, 20, 24, 28, 32, 36, 40
PLAIN, TURNED, LOWER, UPPER = range(4)
ROWS = 16


def dot(a, b, ca, cb):
    return lax.dot_general(a, b, (((ca,), (cb,)), ((), ())), preferred_element_type=F32)


def pieces(x, count):
    out = []
    for _ in range(count):
        piece = x.astype(BF16)
        out.append(piece)
        x = x - piece.astype(F32)
    return out


def where(cond, a, b):
    return jnp.where(cond, a, b)


class Place:
    def __init__(self, index):
        self.row, self.col = lax.axis_index("row"), lax.axis_index("col")
        self.k, self.y = lax.rem(self.col, 2), lax.div(self.col, 2)
        self.q = [index[0], index[1]]
        self.half = [lax.div(q, 2) for q in self.q]
        self.low = [lax.rem(q, 2) for q in self.q]
        self.equal = self.q[0] == self.q[1]
        self.apart = self.half[0] != self.half[1]
        self.together = jnp.logical_not(self.equal | self.apart)
        self.in_row = [self.row == h for h in self.half]
        self.in_col = [self.y == h for h in self.half]

    def tile(self, panel_low, a, s):
        return 2 * (2 * panel_low + a) + s

    def sends(self, n):
        k = self.k
        s, a = n // 2, n % 2
        low = where(self.apart & (self.half[0] != self.row), self.low[1], self.low[0])
        first = self.low[0] == k
        source = [
            where(first, self.tile(1 - k, 0, 0), self.tile(1 - k, 0, 1)),
            where(first, self.tile(1 - k, 0, 1), self.tile(1 - k, 1, 1)),
            self.tile(k, 0, 0),
            self.tile(k, 1, 0),
        ][n]
        both = where(self.in_row[0], self.tile(1 - k, a, s), 2 * (2 * k + s) + a)
        both = where(self.in_row[0] & self.in_col[0], source, both)
        return where(self.together, both, self.tile(low, a, s))

    def message(self, over_row, k):
        first = k == 0 if over_row else k != 0
        return where(k == self.k, where(first, FIRST, SECOND), where(first, FIRST_SIB, SECOND_SIB))

    def passed(self, k):
        return where(k == self.k, PASSED, PASSED_SIB)

    def square(self, base, i, j):
        if i == j:
            return base, jnp.int32(UPPER if i else LOWER)
        return base + 1, jnp.int32(PLAIN if i else TURNED)

    def diagonal(self, over_row, p, i, j):
        return self.square(self.message(over_row, self.low[p]) + 2, i, j)

    def mixed(self, over_row, i, j):
        return self.message(over_row, self.low[i]) + j, jnp.int32(i)

    def pick(self, cond, a, b):
        return where(cond, a[0], b[0]), where(cond, a[1], b[1])

    def rows(self, p, t, s, a):
        here = where(self.q[p] == self.col, OWN, SIB) + 2 * (2 * t + s) + a, jnp.int32(0)
        plain = self.message(False, jnp.int32(t)) + 2 * s + a, jnp.int32(1)
        own = self.square(self.message(False, jnp.int32(t)), s, a)
        plain = self.pick(self.equal & (self.low[p] == t), own, plain)
        same = self.diagonal(False, p, s, a)
        if p == 0:
            cross = self.mixed(False, s, a)
        else:
            cross = self.mixed(False, a, s)
            cross = cross[0], 1 - cross[1]
        both = self.pick(self.low[p] == t, same, cross)
        beside = self.pick(self.together, both, plain)
        passed = self.message(True, jnp.int32(t)) + 2 * s + a, jnp.int32(1)
        kept = self.message(False, jnp.int32(t)) + 2 * s + a, jnp.int32(0)
        far = self.pick(self.together & (self.low[p] == t), kept, passed)
        return self.pick(self.in_col[p], here, self.pick(self.in_row[p], beside, far))

    def cols(self, p, a, s):
        here = self.tile(self.low[p], a, s), jnp.int32(0)
        plain = self.message(True, self.k) + 2 * s + a, jnp.int32(0)
        own = self.square(self.message(True, self.k), a, s)
        plain = self.pick(self.equal & self.in_col[p] & (self.low[p] == self.k), own, plain)
        kept = self.message(False, self.k) + 2 * s + a, jnp.int32(1)
        passed = self.pick(self.low[p] == self.k, kept, plain)
        same = self.diagonal(True, p, a, s)
        if p == 0:
            cross = self.mixed(True, s, a)
            cross = cross[0], 1 - cross[1]
        else:
            cross = self.mixed(True, a, s)
        source = self.pick(self.low[p] == self.k, same, cross)
        both = self.pick(self.in_col[p], source, passed)
        far = self.pick(self.together, both, plain)
        return self.pick(self.in_row[p], here, far)

    def cross(self, i, a):
        mine = self.pick(self.low[1] == 0, self.rows(0, 0, i, a), self.rows(0, 1, i, a))
        turned = self.pick(self.low[0] == 0, self.rows(1, 0, a, i), self.rows(1, 1, a, i))
        turned = turned[0], 1 - turned[1]
        equal_near = self.square(self.message(True, self.low[1]), i, a)
        near = self.pick(self.equal, equal_near, self.mixed(True, i, a))
        equal_far = self.square(self.passed(self.low[0]), i, a)
        both_far = self.passed(self.low[i]) + a, jnp.int32(i)
        far = self.pick(self.equal, equal_far, both_far)
        outside = self.pick(self.in_col[1], near, far)
        return self.pick(self.in_row[1], mine, self.pick(self.in_row[0], turned, outside))


def quarter_of(tile, number, size):
    down = pl.multiple_of(lax.div(number, 2) * size, size)
    along = pl.multiple_of(lax.rem(number, 2) * size, size)
    return tile[pl.ds(down, size), pl.ds(along, size)]


def tie_kernel(_, __, ___):
    pass


TOKEN = jax.ShapeDtypeStruct((8, 128), F32)


def tie(x, *after, params=PARAMS):
    for other in after:
        x = pl.pallas_call(
            tie_kernel,
            out_shape=jax.ShapeDtypeStruct(x.shape, x.dtype),
            in_specs=[ANY, ANY],
            out_specs=ANY,
            input_output_aliases={0: 0},
            compiler_params=params,
        )(x, other)
    return x


def first_kernel(index_far, working, obs_far, rotation_far, order_far, message, own, *rest):
    sent, (index, tile, obs, rotation, order, moved, sems) = rest[:-7], rest[-7:]
    pairs = (
        (order_far, order),
        (rotation_far, rotation),
        (obs_far, obs),
        (index_far, index),
        (working, tile),
    )
    copies = [pltpu.make_async_copy(far, near, sems.at[n]) for n, (far, near) in enumerate(pairs)]
    for copy in copies:
        copy.start()
    row, latent = lax.axis_index("row"), lax.axis_index("latent")
    times, own_vars, stations = obs.shape
    latents, all_vars = rotation.shape
    copies[0].wait()
    local = order[...] - row * stations
    spread = lax.broadcasted_iota(jnp.int32, (stations, stations), 0) == local
    spread = spread.astype(F32).astype(BF16)
    copies[1].wait()
    shape = (latents * times, times * own_vars)
    left = lax.broadcasted_iota(jnp.int32, shape, 0)
    right = lax.broadcasted_iota(jnp.int32, shape, 1)
    keep = lax.rem(left, times) == lax.div(right, own_vars)
    sel_l = lax.broadcasted_iota(jnp.int32, (latents * times, latents), 0)
    sel_l = lax.div(sel_l, times) == lax.broadcasted_iota(jnp.int32, (latents * times, latents), 1)
    pick_v = lax.broadcasted_iota(jnp.int32, (all_vars, times * own_vars), 1)
    pick_v = lax.rem(pick_v, own_vars) + latent * own_vars
    pick_v = pick_v == lax.broadcasted_iota(jnp.int32, (all_vars, times * own_vars), 0)
    sel_l = sel_l.astype(F32).astype(BF16)
    pick_v = pick_v.astype(F32).astype(BF16)
    lefts = []
    for piece in pieces(rotation[...], 3):
        wide = dot(sel_l, piece, 1, 0).astype(BF16)
        wide = dot(wide, pick_v, 1, 0)
        lefts.append(jnp.where(keep, wide, 0.0).astype(BF16))
    copies[2].wait()
    flat = obs[...].reshape(times * own_vars, stations)
    total = sum(dot(wide, flat, 1, 0) for wide in lefts)
    moved[...] = dot(total.astype(BF16), spread, 1, 0).reshape(moved.shape)
    own[...] = moved[latent]
    for shift, out in enumerate(sent, 1):
        out[...] = moved[lax.rem(latent + shift, latents)].astype(BF16)
    copies[3].wait()
    here = Place(index)
    copies[4].wait()
    size = message.shape[1]
    starts = [0, size, 2 * size + ROWS, 3 * size + ROWS]
    for n, start in enumerate(starts):
        message[pl.ds(start, size)] = quarter_of(tile, here.sends(n), size)
    upper = quarter_of(tile, here.tile(here.k, 1, 1), size).astype(F32)
    down = lax.broadcasted_iota(jnp.int32, (size, size), 0)
    along = lax.broadcasted_iota(jnp.int32, (size, size), 1)
    triangles = jnp.where(down >= along, quarter_of(tile, here.tile(here.k, 0, 0), size).astype(F32), upper).astype(BF16)
    middle = jnp.sum(jnp.where(down == along, upper, 0.0), axis=0, keepdims=True)
    message[pl.ds(2 * size, ROWS)] = jnp.broadcast_to(middle, (ROWS, size)).astype(BF16)
    source = here.in_row[0] & here.in_col[0]

    @pl.when(source & here.equal & (here.low[0] == here.k))
    def _():
        message[pl.ds(starts[0], size)] = triangles

    @pl.when(source & here.together)
    def _():
        message[pl.ds(starts[2], size)] = triangles


def field_kernel(index, own, *rest):
    got, (field, rhs) = rest[:-2], rest[-2:]
    total = own[...]
    for part in got:
        total = total + part[...].astype(F32)
    field[...] = total
    width = rhs.shape[2]
    for p in range(rhs.shape[0]):
        inside = pl.ds(pl.multiple_of(lax.rem(index[p], 2) * width, width), width)
        rhs[p] = field[:, inside].astype(BF16)


def entries_of(here):
    entries = []
    for p in range(2):
        entries += [here.rows(p, n // 4, n // 2 % 2, n % 2) for n in range(8)]
    for p in range(2):
        entries += [here.cols(p, n // 2, n % 2) for n in range(4)]
    return entries + [here.cross(n // 2, n % 2) for n in range(4)]


def is_late(slot):
    return slot >= SECOND


def assemble(blocks, pool, middles, table, flip, base, wanted, earlier=None):
    size = pool.shape[1]

    def step(n, _):
        down = pl.ds(pl.multiple_of(n * size, size), size)
        for side in range(2):
            slot = table[2 * n + side]
            turn = flip[2 * n + side]
            along = pl.ds(side * size, size)
            here = wanted(slot)

            if earlier is not None:

                @pl.when(jnp.logical_not(here))
                def _():
                    blocks[down, along] = earlier[down, along]

            @pl.when(here & (turn == PLAIN))
            def _():
                blocks[down, along] = pool[slot - base]

            @pl.when(here & (turn == TURNED))
            def _():
                blocks[down, along] = pool[slot - base].T

            @pl.when(here & (turn >= LOWER))
            def _():
                both = pool[slot - base].astype(F32)
                i = lax.broadcasted_iota(jnp.int32, (size, size), 0)
                j = lax.broadcasted_iota(jnp.int32, (size, size), 1)
                lower = jnp.where(i >= j, both, both.T)
                middle = middles[lax.div(slot - base, 4)].astype(F32)[0:1]
                upper = jnp.where(i == j, middle, jnp.where(i < j, both, both.T))
                blocks[down, along] = jnp.where(turn == LOWER, lower, upper).astype(BF16)

        return 0

    lax.fori_loop(0, blocks.shape[0] // size, step, 0)


def unpack(ref, pool, middles, slot, number):
    size = pool.shape[1]
    pool[slot] = ref[pl.ds(0, size)]
    pool[slot + 1] = ref[pl.ds(size, size)]
    middles[number] = ref[pl.ds(2 * size, ROWS)]
    if ref.shape[0] > 3 * size:
        pool[slot + 2] = ref[pl.ds(2 * size + ROWS, size)]
        pool[slot + 3] = ref[pl.ds(3 * size + ROWS, size)]


def early_kernel(index, working, sibling, first, first_sib, blocks, table, flip, pool, middles):
    here = Place(index)
    size = pool.shape[1]
    for n, (slot, turn) in enumerate(entries_of(here)):
        table[n] = slot
        flip[n] = turn

    def tiles(n, _):
        down = pl.ds(pl.multiple_of(n * size, size), size)
        for side in range(2):
            along = pl.ds(side * size, size)
            pool[OWN + 2 * n + side] = working[down, along]
            pool[SIB + 2 * n + side] = sibling[down, along]
        return 0

    lax.fori_loop(0, working.shape[0] // size, tiles, 0)
    unpack(first, pool, middles, FIRST, FIRST // 4)
    unpack(first_sib, pool, middles, FIRST_SIB, FIRST_SIB // 4)
    assemble(blocks, pool, middles, table, flip, 0, lambda slot: jnp.logical_not(is_late(slot)))


def factor_kernel(
    index, table, flip, working, earlier, second, second_sib, passed, passed_sib,
    inverse, field, rhs_far, trailing, panels, whitened,
    blocks, pool, middles, factors0, factors1, turned0, turned1, rhs_near, result, sems,
):
    here = Place(index)
    size = pool.shape[1]
    tall, wide = working.shape
    width = inverse.shape[1]
    share = panels.shape[2]

    for n, ref in enumerate((second, second_sib, passed, passed_sib)):
        unpack(ref, pool, middles, 4 * n, n)
    assemble(blocks, pool, middles, table, flip, SECOND, is_late, earlier)

    rows0, rows1 = pl.ds(0, tall), pl.ds(tall, tall)
    cols0, cols1 = pl.ds(2 * tall, width), pl.ds(2 * tall + width, width)
    cross = pl.ds(2 * tall + 2 * width, width)
    inv0, inv1 = inverse[0], inverse[1]

    factors0[pl.ds(tall, width)] = dot(blocks[cross], inv0, 1, 1).astype(BF16)
    turned0[...] = dot(inv0, blocks[cols0], 1, 0).astype(BF16)
    factors0[rows0] = dot(blocks[rows0], inv0, 1, 1).astype(BF16)
    mixed = factors0[pl.ds(tall, width)]

    got = blocks[cols1].astype(F32) - dot(mixed, turned0[...], 1, 0)
    turned1[...] = dot(inv1, got.astype(BF16), 1, 0).astype(BF16)
    got = blocks[rows1].astype(F32) - dot(factors0[rows0], mixed, 1, 1)
    factors1[...] = dot(got.astype(BF16), inv1, 1, 1).astype(BF16)

    lanes = pl.ds(pl.multiple_of(here.col * share, share), share)
    copies = [
        pltpu.make_async_copy(factors0.at[rows0, lanes], panels.at[0], sems.at[0]),
        pltpu.make_async_copy(factors1.at[:, lanes], panels.at[1], sems.at[1]),
    ]
    copies[0].start()
    copies[1].start()
    parts = sems.shape[0] - 2
    for n in range(parts):
        down = pl.ds(n * tall // parts, tall // parts)
        change = dot(factors0[down], turned0[...], 1, 0) + dot(factors1[down], turned1[...], 1, 0)
        result[down] = working[down].astype(F32) - change
        copies.append(pltpu.make_async_copy(result.at[down], trailing.at[down], sems.at[2 + n]))
        copies[-1].start()

    for p in range(2):
        inside = pl.ds(pl.multiple_of(here.low[p] * width, width), width)

        @pl.when(here.in_row[p])
        def _():
            rhs_near[p] = field[:, inside]

        @pl.when(jnp.logical_not(here.in_row[p]))
        def _():
            rhs_near[p] = rhs_far[p].astype(F32)

    def solve(rhs, inv):
        return sum(dot(piece, inv, 1, 1) for piece in pieces(rhs, 2)).astype(BF16)

    solved0 = solve(rhs_near[0], inv0)
    solved1 = solve(rhs_near[1] - dot(solved0, mixed, 1, 1), inv1)
    whitened[...] = field[...] - dot(solved0, factors0[rows0], 1, 1) - dot(solved1, factors1[...], 1, 1)
    for copy in copies:
        copy.wait()


def local(observations, rotation, ordering, working, factor_inverse, panel_index):
    latents = rotation.shape[1]
    latent_count = lax.axis_size("latent")
    times, own_vars, stations = observations.shape
    matrix = working[0]
    inverse = factor_inverse[0]
    tall, wide = matrix.shape
    panel_count, width, _ = inverse.shape
    size = width // 2
    share = width // lax.axis_size("col")

    cols = lax.axis_size("col")

    def across_rows(x):
        return lax.ppermute(x, "row", [(0, 1), (1, 0)])

    def siblings(x):
        return lax.ppermute(x, "col", [(i, i ^ 1) for i in range(cols)])

    def neighbours(x, row_first):
        pairs = []
        for i in range(2):
            for j in range(cols):
                over_row = (j % 2 == 0) == row_first
                to = (1 - i, j) if over_row else (i, j ^ 2)
                pairs.append((i * cols + j, to[0] * cols + to[1]))
        return lax.ppermute(x, ("row", "col"), pairs)

    message = jax.ShapeDtypeStruct((4 * size + ROWS, size), BF16)
    sibling = siblings(matrix)
    sent_message, own, *sent = pl.pallas_call(
        first_kernel,
        out_shape=[message, jax.ShapeDtypeStruct((times, stations), F32)]
        + [jax.ShapeDtypeStruct((times, stations), BF16)] * (latent_count - 1),
        in_specs=[ANY] * 5,
        out_specs=[VMEM] * (1 + latent_count),
        scratch_shapes=[
            pltpu.SMEM(panel_index.shape, jnp.int32),
            pltpu.VMEM(matrix.shape, BF16),
            pltpu.VMEM(observations.shape, BF16),
            pltpu.VMEM(rotation.shape[::-1], F32),
            pltpu.VMEM((1, stations), jnp.int32),
            pltpu.VMEM((latents, times, stations), F32),
            pltpu.SemaphoreType.DMA((5,)),
        ],
        compiler_params=WIDE,
    )(panel_index, matrix, observations, rotation.T, ordering[None])
    first = neighbours(sent_message, True)
    got = []
    for shift, part in enumerate(sent, 1):
        pairs = [(i, (i + shift) % latent_count) for i in range(latent_count)]
        got.append(lax.ppermute(part, "latent", pairs))

    second = neighbours(sent_message, False)
    first = tie(first, *got)
    field, rhs = pl.pallas_call(
        field_kernel,
        out_shape=(
            jax.ShapeDtypeStruct((times, stations), F32),
            jax.ShapeDtypeStruct((panel_count, times, width), BF16),
        ),
        in_specs=[SMEM] + [VMEM] * latent_count,
        out_specs=(VMEM, VMEM),
        compiler_params=PARAMS,
    )(panel_index, own, *got)
    rhs_far = across_rows(rhs)
    first_sib = siblings(first)
    passed = neighbours(first[: 2 * size + ROWS], False)
    block_shape = jax.ShapeDtypeStruct((14 * size, width), BF16)
    table_shape = jax.ShapeDtypeStruct((28,), jnp.int32)
    blocks, table, flip = pl.pallas_call(
        early_kernel,
        out_shape=(block_shape, table_shape, table_shape),
        in_specs=[SMEM] + [VMEM] * 4,
        out_specs=(VMEM, SMEM, SMEM),
        scratch_shapes=[
            pltpu.VMEM((SECOND, size, size), BF16),
            pltpu.VMEM((SECOND // 4, ROWS, size), BF16),
        ],
        compiler_params=PARAMS,
    )(panel_index, matrix, sibling, first, first_sib)

    second = tie(second, rhs_far)
    second_sib, passed_sib = siblings(second), siblings(passed)

    trailing, panels, whitened = pl.pallas_call(
        factor_kernel,
        out_shape=(
            jax.ShapeDtypeStruct((tall, wide), F32),
            jax.ShapeDtypeStruct((panel_count, tall, share), BF16),
            jax.ShapeDtypeStruct((times, stations), F32),
        ),
        in_specs=[SMEM] * 3 + [VMEM] * 9,
        out_specs=(HBM, HBM, VMEM),
        scratch_shapes=[
            pltpu.VMEM(block_shape.shape, BF16),
            pltpu.VMEM((POOL - SECOND, size, size), BF16),
            pltpu.VMEM(((POOL - SECOND) // 4, ROWS, size), BF16),
            pltpu.VMEM((tall + width, width), BF16),
            pltpu.VMEM((tall, width), BF16),
            pltpu.VMEM((width, wide), BF16),
            pltpu.VMEM((width, wide), BF16),
            pltpu.VMEM((panel_count, times, width), F32),
            pltpu.VMEM((tall, wide), F32),
            pltpu.SemaphoreType.DMA((4,)),
        ],
        compiler_params=PARAMS,
    )(
        panel_index, table, flip, matrix, blocks, second, second_sib, passed, passed_sib,
        inverse, field, rhs_far,
    )
    return trailing[None], panels[None], whitened[None]


def solution(mesh):
    return jax.shard_map(
        local,
        mesh=mesh,
        in_specs=(
            P("col", "latent", "row"),
            P(),
            P("row"),
            P("latent", "row", "col"),
            P("latent", None, None, None),
            P(),
        ),
        out_specs=(
            P("latent", "row", "col"),
            P("latent", None, "row", "col"),
            P("latent", "col", "row"),
        ),
        check_vma=False,
    )
```

```python
import jax
import jax.numpy as jnp
from jax import lax
from jax.experimental import pallas as pl
from jax.experimental.pallas import tpu as pltpu
from jax.sharding import PartitionSpec as P

F32 = jnp.float32
BF16 = jnp.bfloat16
VMEM = pl.BlockSpec(memory_space=pltpu.VMEM)
SMEM = pl.BlockSpec(memory_space=pltpu.SMEM)
ANY = pl.BlockSpec(memory_space=pl.ANY)
HBM = pl.BlockSpec(memory_space=pltpu.HBM)
PARAMS = pltpu.CompilerParams(vmem_limit_bytes=24 * 1024 * 1024)
WIDE = pltpu.CompilerParams(vmem_limit_bytes=60 * 1024 * 1024)

OWN, SIB, FIRST, FIRST_SIB, SECOND, SECOND_SIB, PASSED, PASSED_SIB, POOL = 0, 8, 16, 20, 24, 28, 32, 36, 40
PLAIN, TURNED, LOWER, UPPER = range(4)
ROWS = 16


def dot(a, b, ca, cb):
    return lax.dot_general(a, b, (((ca,), (cb,)), ((), ())), preferred_element_type=F32)


def by_lower(x, inverse, out, rows):
    half = inverse.shape[0] // 2
    out[rows, :half] = dot(x[:, :half], inverse[:half, :half], 1, 1).astype(BF16)
    out[rows, half:] = dot(x, inverse[half:], 1, 1).astype(BF16)


def lower_by(inverse, x, out):
    half = inverse.shape[0] // 2
    out[:half] = dot(inverse[:half, :half], x[:half], 1, 0).astype(BF16)
    out[half:] = dot(inverse[half:], x, 1, 0).astype(BF16)


def pieces(x, count):
    out = []
    for _ in range(count):
        piece = x.astype(BF16)
        out.append(piece)
        x = x - piece.astype(F32)
    return out


def where(cond, a, b):
    return jnp.where(cond, a, b)


class Place:
    def __init__(self, index):
        self.row, self.col = lax.axis_index("row"), lax.axis_index("col")
        self.k, self.y = lax.rem(self.col, 2), lax.div(self.col, 2)
        self.q = [index[0], index[1]]
        self.half = [lax.div(q, 2) for q in self.q]
        self.low = [lax.rem(q, 2) for q in self.q]
        self.equal = self.q[0] == self.q[1]
        self.apart = self.half[0] != self.half[1]
        self.together = jnp.logical_not(self.equal | self.apart)
        self.in_row = [self.row == h for h in self.half]
        self.in_col = [self.y == h for h in self.half]

    def tile(self, panel_low, a, s):
        return 2 * (2 * panel_low + a) + s

    def sends(self, n):
        k = self.k
        s, a = n // 2, n % 2
        low = where(self.apart & (self.half[0] != self.row), self.low[1], self.low[0])
        first = self.low[0] == k
        source = [
            where(first, self.tile(1 - k, 0, 0), self.tile(1 - k, 0, 1)),
            where(first, self.tile(1 - k, 0, 1), self.tile(1 - k, 1, 1)),
            self.tile(k, 0, 0),
            self.tile(k, 1, 0),
        ][n]
        both = where(self.in_row[0], self.tile(1 - k, a, s), 2 * (2 * k + s) + a)
        both = where(self.in_row[0] & self.in_col[0], source, both)
        return where(self.together, both, self.tile(low, a, s))

    def message(self, over_row, k):
        first = k == 0 if over_row else k != 0
        return where(k == self.k, where(first, FIRST, SECOND), where(first, FIRST_SIB, SECOND_SIB))

    def passed(self, k):
        return where(k == self.k, PASSED, PASSED_SIB)

    def square(self, base, i, j):
        if i == j:
            return base, jnp.int32(UPPER if i else LOWER)
        return base + 1, jnp.int32(PLAIN if i else TURNED)

    def diagonal(self, over_row, p, i, j):
        return self.square(self.message(over_row, self.low[p]) + 2, i, j)

    def mixed(self, over_row, i, j):
        return self.message(over_row, self.low[i]) + j, jnp.int32(i)

    def pick(self, cond, a, b):
        return where(cond, a[0], b[0]), where(cond, a[1], b[1])

    def rows(self, p, t, s, a):
        here = where(self.q[p] == self.col, OWN, SIB) + 2 * (2 * t + s) + a, jnp.int32(0)
        plain = self.message(False, jnp.int32(t)) + 2 * s + a, jnp.int32(1)
        own = self.square(self.message(False, jnp.int32(t)), s, a)
        plain = self.pick(self.equal & (self.low[p] == t), own, plain)
        same = self.diagonal(False, p, s, a)
        if p == 0:
            cross = self.mixed(False, s, a)
        else:
            cross = self.mixed(False, a, s)
            cross = cross[0], 1 - cross[1]
        both = self.pick(self.low[p] == t, same, cross)
        beside = self.pick(self.together, both, plain)
        passed = self.message(True, jnp.int32(t)) + 2 * s + a, jnp.int32(1)
        kept = self.message(False, jnp.int32(t)) + 2 * s + a, jnp.int32(0)
        far = self.pick(self.together & (self.low[p] == t), kept, passed)
        return self.pick(self.in_col[p], here, self.pick(self.in_row[p], beside, far))

    def cols(self, p, a, s):
        here = self.tile(self.low[p], a, s), jnp.int32(0)
        plain = self.message(True, self.k) + 2 * s + a, jnp.int32(0)
        own = self.square(self.message(True, self.k), a, s)
        plain = self.pick(self.equal & self.in_col[p] & (self.low[p] == self.k), own, plain)
        kept = self.message(False, self.k) + 2 * s + a, jnp.int32(1)
        passed = self.pick(self.low[p] == self.k, kept, plain)
        same = self.diagonal(True, p, a, s)
        if p == 0:
            cross = self.mixed(True, s, a)
            cross = cross[0], 1 - cross[1]
        else:
            cross = self.mixed(True, a, s)
        source = self.pick(self.low[p] == self.k, same, cross)
        both = self.pick(self.in_col[p], source, passed)
        far = self.pick(self.together, both, plain)
        return self.pick(self.in_row[p], here, far)

    def cross(self, i, a):
        mine = self.pick(self.low[1] == 0, self.rows(0, 0, i, a), self.rows(0, 1, i, a))
        turned = self.pick(self.low[0] == 0, self.rows(1, 0, a, i), self.rows(1, 1, a, i))
        turned = turned[0], 1 - turned[1]
        equal_near = self.square(self.message(True, self.low[1]), i, a)
        near = self.pick(self.equal, equal_near, self.mixed(True, i, a))
        equal_far = self.square(self.passed(self.low[0]), i, a)
        both_far = self.passed(self.low[i]) + a, jnp.int32(i)
        far = self.pick(self.equal, equal_far, both_far)
        outside = self.pick(self.in_col[1], near, far)
        return self.pick(self.in_row[1], mine, self.pick(self.in_row[0], turned, outside))


def quarter_of(tile, number, size):
    down = pl.multiple_of(lax.div(number, 2) * size, size)
    along = pl.multiple_of(lax.rem(number, 2) * size, size)
    return tile[pl.ds(down, size), pl.ds(along, size)]


def tie_kernel(_, __, ___):
    pass


TOKEN = jax.ShapeDtypeStruct((8, 128), F32)


def tie(x, *after, params=PARAMS):
    for other in after:
        x = pl.pallas_call(
            tie_kernel,
            out_shape=jax.ShapeDtypeStruct(x.shape, x.dtype),
            in_specs=[ANY, ANY],
            out_specs=ANY,
            input_output_aliases={0: 0},
            compiler_params=params,
        )(x, other)
    return x


def first_kernel(index_far, working, obs_far, rotation_far, order_far, message, own, *rest):
    sent, (index, tile, obs, rotation, order, moved, sems) = rest[:-7], rest[-7:]
    pairs = (
        (order_far, order),
        (rotation_far, rotation),
        (obs_far, obs),
        (index_far, index),
        (working, tile),
    )
    copies = [pltpu.make_async_copy(far, near, sems.at[n]) for n, (far, near) in enumerate(pairs)]
    for copy in copies:
        copy.start()
    row, latent = lax.axis_index("row"), lax.axis_index("latent")
    times, own_vars, stations = obs.shape
    latents, all_vars = rotation.shape
    copies[0].wait()
    local = order[...] - row * stations
    spread = lax.broadcasted_iota(jnp.int32, (stations, stations), 0) == local
    spread = spread.astype(F32).astype(BF16)
    copies[1].wait()
    shape = (latents * times, times * own_vars)
    left = lax.broadcasted_iota(jnp.int32, shape, 0)
    right = lax.broadcasted_iota(jnp.int32, shape, 1)
    keep = lax.rem(left, times) == lax.div(right, own_vars)
    sel_l = lax.broadcasted_iota(jnp.int32, (latents * times, latents), 0)
    sel_l = lax.div(sel_l, times) == lax.broadcasted_iota(jnp.int32, (latents * times, latents), 1)
    pick_v = lax.broadcasted_iota(jnp.int32, (all_vars, times * own_vars), 1)
    pick_v = lax.rem(pick_v, own_vars) + latent * own_vars
    pick_v = pick_v == lax.broadcasted_iota(jnp.int32, (all_vars, times * own_vars), 0)
    sel_l = sel_l.astype(F32).astype(BF16)
    pick_v = pick_v.astype(F32).astype(BF16)
    lefts = []
    for piece in pieces(rotation[...], 3):
        wide = dot(sel_l, piece, 1, 0).astype(BF16)
        wide = dot(wide, pick_v, 1, 0)
        lefts.append(jnp.where(keep, wide, 0.0).astype(BF16))
    copies[2].wait()
    flat = obs[...].reshape(times * own_vars, stations)
    total = sum(dot(wide, flat, 1, 0) for wide in lefts)
    moved[...] = dot(total.astype(BF16), spread, 1, 0).reshape(moved.shape)
    own[...] = moved[latent]
    for shift, out in enumerate(sent, 1):
        out[...] = moved[lax.rem(latent + shift, latents)].astype(BF16)
    copies[3].wait()
    here = Place(index)
    copies[4].wait()
    size = message.shape[1]
    starts = [0, size, 2 * size + ROWS, 3 * size + ROWS]
    for n, start in enumerate(starts):
        message[pl.ds(start, size)] = quarter_of(tile, here.sends(n), size)
    upper = quarter_of(tile, here.tile(here.k, 1, 1), size).astype(F32)
    down = lax.broadcasted_iota(jnp.int32, (size, size), 0)
    along = lax.broadcasted_iota(jnp.int32, (size, size), 1)
    triangles = jnp.where(down >= along, quarter_of(tile, here.tile(here.k, 0, 0), size).astype(F32), upper).astype(BF16)
    middle = jnp.sum(jnp.where(down == along, upper, 0.0), axis=0, keepdims=True)
    message[pl.ds(2 * size, ROWS)] = jnp.broadcast_to(middle, (ROWS, size)).astype(BF16)
    source = here.in_row[0] & here.in_col[0]

    @pl.when(source & here.equal & (here.low[0] == here.k))
    def _():
        message[pl.ds(starts[0], size)] = triangles

    @pl.when(source & here.together)
    def _():
        message[pl.ds(starts[2], size)] = triangles


def field_kernel(index, own, *rest):
    got, (field, rhs) = rest[:-2], rest[-2:]
    total = own[...]
    for part in got:
        total = total + part[...].astype(F32)
    field[...] = total
    width = rhs.shape[2]
    for p in range(rhs.shape[0]):
        inside = pl.ds(pl.multiple_of(lax.rem(index[p], 2) * width, width), width)
        rhs[p] = field[:, inside].astype(BF16)


def entries_of(here):
    entries = []
    for p in range(2):
        entries += [here.rows(p, n // 4, n // 2 % 2, n % 2) for n in range(8)]
    for p in range(2):
        entries += [here.cols(p, n // 2, n % 2) for n in range(4)]
    return entries + [here.cross(n // 2, n % 2) for n in range(4)]


def is_late(slot):
    return slot >= SECOND


def assemble(blocks, pool, middles, table, flip, base, wanted, earlier=None):
    size = pool.shape[1]

    def step(n, _):
        down = pl.ds(pl.multiple_of(n * size, size), size)
        for side in range(2):
            slot = table[2 * n + side]
            turn = flip[2 * n + side]
            along = pl.ds(side * size, size)
            here = wanted(slot)

            if earlier is not None:

                @pl.when(jnp.logical_not(here))
                def _():
                    blocks[down, along] = earlier[down, along]

            @pl.when(here & (turn == PLAIN))
            def _():
                blocks[down, along] = pool[slot - base]

            @pl.when(here & (turn == TURNED))
            def _():
                blocks[down, along] = pool[slot - base].T

            @pl.when(here & (turn >= LOWER))
            def _():
                both = pool[slot - base].astype(F32)
                i = lax.broadcasted_iota(jnp.int32, (size, size), 0)
                j = lax.broadcasted_iota(jnp.int32, (size, size), 1)
                lower = jnp.where(i >= j, both, both.T)
                middle = middles[lax.div(slot - base, 4)].astype(F32)[0:1]
                upper = jnp.where(i == j, middle, jnp.where(i < j, both, both.T))
                blocks[down, along] = jnp.where(turn == LOWER, lower, upper).astype(BF16)

        return 0

    lax.fori_loop(0, blocks.shape[0] // size, step, 0)


def unpack(ref, pool, middles, slot, number):
    size = pool.shape[1]
    pool[slot] = ref[pl.ds(0, size)]
    pool[slot + 1] = ref[pl.ds(size, size)]
    middles[number] = ref[pl.ds(2 * size, ROWS)]
    if ref.shape[0] > 3 * size:
        pool[slot + 2] = ref[pl.ds(2 * size + ROWS, size)]
        pool[slot + 3] = ref[pl.ds(3 * size + ROWS, size)]


def early_kernel(index, working, sibling, first, first_sib, blocks, table, flip, pool, middles):
    here = Place(index)
    size = pool.shape[1]
    for n, (slot, turn) in enumerate(entries_of(here)):
        table[n] = slot
        flip[n] = turn

    def tiles(n, _):
        down = pl.ds(pl.multiple_of(n * size, size), size)
        for side in range(2):
            along = pl.ds(side * size, size)
            pool[OWN + 2 * n + side] = working[down, along]
            pool[SIB + 2 * n + side] = sibling[down, along]
        return 0

    lax.fori_loop(0, working.shape[0] // size, tiles, 0)
    unpack(first, pool, middles, FIRST, FIRST // 4)
    unpack(first_sib, pool, middles, FIRST_SIB, FIRST_SIB // 4)
    assemble(blocks, pool, middles, table, flip, 0, lambda slot: jnp.logical_not(is_late(slot)))


def factor_kernel(
    index, table, flip, working, earlier, second, second_sib, passed, passed_sib,
    inverse, field, rhs_far, trailing, panels, whitened,
    blocks, pool, middles, factors0, factors1, turned0, turned1, rhs_near, result, sems,
):
    here = Place(index)
    size = pool.shape[1]
    tall, wide = working.shape
    width = inverse.shape[1]
    share = panels.shape[2]

    for n, ref in enumerate((second, second_sib, passed, passed_sib)):
        unpack(ref, pool, middles, 4 * n, n)
    assemble(blocks, pool, middles, table, flip, SECOND, is_late, earlier)

    rows0, rows1 = pl.ds(0, tall), pl.ds(tall, tall)
    cols0, cols1 = pl.ds(2 * tall, width), pl.ds(2 * tall + width, width)
    cross = pl.ds(2 * tall + 2 * width, width)
    inv0, inv1 = inverse[0], inverse[1]

    by_lower(blocks[cross], inv0, factors0, slice(tall, tall + width))
    lower_by(inv0, blocks[cols0], turned0)
    by_lower(blocks[rows0], inv0, factors0, slice(0, tall))
    mixed = factors0[pl.ds(tall, width)]

    got = blocks[cols1].astype(F32) - dot(mixed, turned0[...], 1, 0)
    lower_by(inv1, got.astype(BF16), turned1)
    got = blocks[rows1].astype(F32) - dot(factors0[rows0], mixed, 1, 1)
    by_lower(got.astype(BF16), inv1, factors1, slice(0, tall))

    lanes = pl.ds(pl.multiple_of(here.col * share, share), share)
    copies = [
        pltpu.make_async_copy(factors0.at[rows0, lanes], panels.at[0], sems.at[0]),
        pltpu.make_async_copy(factors1.at[:, lanes], panels.at[1], sems.at[1]),
    ]
    copies[0].start()
    copies[1].start()
    parts = sems.shape[0] - 2
    for n in range(parts):
        down = pl.ds(n * tall // parts, tall // parts)
        change = dot(factors0[down], turned0[...], 1, 0) + dot(factors1[down], turned1[...], 1, 0)
        result[down] = working[down].astype(F32) - change
        copies.append(pltpu.make_async_copy(result.at[down], trailing.at[down], sems.at[2 + n]))
        copies[-1].start()

    for p in range(2):
        inside = pl.ds(pl.multiple_of(here.low[p] * width, width), width)

        @pl.when(here.in_row[p])
        def _():
            rhs_near[p] = field[:, inside]

        @pl.when(jnp.logical_not(here.in_row[p]))
        def _():
            rhs_near[p] = rhs_far[p].astype(F32)

    def solve(rhs, inv):
        return sum(dot(piece, inv, 1, 1) for piece in pieces(rhs, 2)).astype(BF16)

    solved0 = solve(rhs_near[0], inv0)
    solved1 = solve(rhs_near[1] - dot(solved0, mixed, 1, 1), inv1)
    whitened[...] = field[...] - dot(solved0, factors0[rows0], 1, 1) - dot(solved1, factors1[...], 1, 1)
    for copy in copies:
        copy.wait()


def local(observations, rotation, ordering, working, factor_inverse, panel_index):
    latents = rotation.shape[1]
    latent_count = lax.axis_size("latent")
    times, own_vars, stations = observations.shape
    matrix = working[0]
    inverse = factor_inverse[0]
    tall, wide = matrix.shape
    panel_count, width, _ = inverse.shape
    size = width // 2
    share = width // lax.axis_size("col")

    cols = lax.axis_size("col")

    def across_rows(x):
        return lax.ppermute(x, "row", [(0, 1), (1, 0)])

    def siblings(x):
        return lax.ppermute(x, "col", [(i, i ^ 1) for i in range(cols)])

    def neighbours(x, row_first):
        pairs = []
        for i in range(2):
            for j in range(cols):
                over_row = (j % 2 == 0) == row_first
                to = (1 - i, j) if over_row else (i, j ^ 2)
                pairs.append((i * cols + j, to[0] * cols + to[1]))
        return lax.ppermute(x, ("row", "col"), pairs)

    message = jax.ShapeDtypeStruct((4 * size + ROWS, size), BF16)
    sibling = siblings(matrix)
    sent_message, own, *sent = pl.pallas_call(
        first_kernel,
        out_shape=[message, jax.ShapeDtypeStruct((times, stations), F32)]
        + [jax.ShapeDtypeStruct((times, stations), BF16)] * (latent_count - 1),
        in_specs=[ANY] * 5,
        out_specs=[VMEM] * (1 + latent_count),
        scratch_shapes=[
            pltpu.SMEM(panel_index.shape, jnp.int32),
            pltpu.VMEM(matrix.shape, BF16),
            pltpu.VMEM(observations.shape, BF16),
            pltpu.VMEM(rotation.shape[::-1], F32),
            pltpu.VMEM((1, stations), jnp.int32),
            pltpu.VMEM((latents, times, stations), F32),
            pltpu.SemaphoreType.DMA((5,)),
        ],
        compiler_params=WIDE,
    )(panel_index, matrix, observations, rotation.T, ordering[None])
    first = neighbours(sent_message, True)
    got = []
    for shift, part in enumerate(sent, 1):
        pairs = [(i, (i + shift) % latent_count) for i in range(latent_count)]
        got.append(lax.ppermute(part, "latent", pairs))

    second = neighbours(sent_message, False)
    first = tie(first, *got)
    field, rhs = pl.pallas_call(
        field_kernel,
        out_shape=(
            jax.ShapeDtypeStruct((times, stations), F32),
            jax.ShapeDtypeStruct((panel_count, times, width), BF16),
        ),
        in_specs=[SMEM] + [VMEM] * latent_count,
        out_specs=(VMEM, VMEM),
        compiler_params=PARAMS,
    )(panel_index, own, *got)
    rhs_far = across_rows(rhs)
    first_sib = siblings(first)
    passed = neighbours(first[: 2 * size + ROWS], False)
    block_shape = jax.ShapeDtypeStruct((14 * size, width), BF16)
    table_shape = jax.ShapeDtypeStruct((28,), jnp.int32)
    blocks, table, flip = pl.pallas_call(
        early_kernel,
        out_shape=(block_shape, table_shape, table_shape),
        in_specs=[SMEM] + [VMEM] * 4,
        out_specs=(VMEM, SMEM, SMEM),
        scratch_shapes=[
            pltpu.VMEM((SECOND, size, size), BF16),
            pltpu.VMEM((SECOND // 4, ROWS, size), BF16),
        ],
        compiler_params=PARAMS,
    )(panel_index, matrix, sibling, first, first_sib)

    second = tie(second, rhs_far, table)
    second_sib, passed_sib = siblings(second), siblings(passed)

    trailing, panels, whitened = pl.pallas_call(
        factor_kernel,
        out_shape=(
            jax.ShapeDtypeStruct((tall, wide), F32),
            jax.ShapeDtypeStruct((panel_count, tall, share), BF16),
            jax.ShapeDtypeStruct((times, stations), F32),
        ),
        in_specs=[SMEM] * 3 + [VMEM] * 9,
        out_specs=(HBM, HBM, VMEM),
        scratch_shapes=[
            pltpu.VMEM(block_shape.shape, BF16),
            pltpu.VMEM((POOL - SECOND, size, size), BF16),
            pltpu.VMEM(((POOL - SECOND) // 4, ROWS, size), BF16),
            pltpu.VMEM((tall + width, width), BF16),
            pltpu.VMEM((tall, width), BF16),
            pltpu.VMEM((width, wide), BF16),
            pltpu.VMEM((width, wide), BF16),
            pltpu.VMEM((panel_count, times, width), F32),
            pltpu.VMEM((tall, wide), F32),
            pltpu.SemaphoreType.DMA((6,)),
        ],
        compiler_params=PARAMS,
    )(
        panel_index, table, flip, matrix, blocks, second, second_sib, passed, passed_sib,
        inverse, field, rhs_far,
    )
    return trailing[None], panels[None], whitened[None]


def solution(mesh):
    return jax.shard_map(
        local,
        mesh=mesh,
        in_specs=(
            P("col", "latent", "row"),
            P(),
            P("row"),
            P("latent", "row", "col"),
            P("latent", None, None, None),
            P(),
        ),
        out_specs=(
            P("latent", "row", "col"),
            P("latent", None, "row", "col"),
            P("latent", "col", "row"),
        ),
        check_vma=False,
    )
```

```python
import jax
import jax.numpy as jnp
from jax import lax
from jax.experimental import pallas as pl
from jax.experimental.pallas import tpu as pltpu
from jax.sharding import PartitionSpec as P

F32 = jnp.float32
BF16 = jnp.bfloat16
VMEM = pl.BlockSpec(memory_space=pltpu.VMEM)
SMEM = pl.BlockSpec(memory_space=pltpu.SMEM)
ANY = pl.BlockSpec(memory_space=pl.ANY)
HBM = pl.BlockSpec(memory_space=pltpu.HBM)
PARAMS = pltpu.CompilerParams(vmem_limit_bytes=24 * 1024 * 1024)
WIDE = pltpu.CompilerParams(vmem_limit_bytes=60 * 1024 * 1024)

OWN, SIB, FIRST, FIRST_SIB, SECOND, SECOND_SIB, PASSED, PASSED_SIB, POOL = 0, 8, 16, 20, 24, 28, 32, 36, 40
PLAIN, TURNED, LOWER, UPPER = range(4)
ROWS = 16


def dot(a, b, ca, cb):
    return lax.dot_general(a, b, (((ca,), (cb,)), ((), ())), preferred_element_type=F32)


def by_lower(x, inverse, out, rows):
    half = inverse.shape[0] // 2
    out[rows, :half] = dot(x[:, :half], inverse[:half, :half], 1, 1).astype(BF16)
    out[rows, half:] = dot(x, inverse[half:], 1, 1).astype(BF16)


def lower_by(inverse, x, out):
    half = inverse.shape[0] // 2
    out[:half] = dot(inverse[:half, :half], x[:half], 1, 0).astype(BF16)
    out[half:] = dot(inverse[half:], x, 1, 0).astype(BF16)


def pieces(x, count):
    out = []
    for _ in range(count):
        piece = x.astype(BF16)
        out.append(piece)
        x = x - piece.astype(F32)
    return out


def where(cond, a, b):
    return jnp.where(cond, a, b)


class Place:
    def __init__(self, index):
        self.row, self.col = lax.axis_index("row"), lax.axis_index("col")
        self.k, self.y = lax.rem(self.col, 2), lax.div(self.col, 2)
        self.q = [index[0], index[1]]
        self.half = [lax.div(q, 2) for q in self.q]
        self.low = [lax.rem(q, 2) for q in self.q]
        self.equal = self.q[0] == self.q[1]
        self.apart = self.half[0] != self.half[1]
        self.together = jnp.logical_not(self.equal | self.apart)
        self.in_row = [self.row == h for h in self.half]
        self.in_col = [self.y == h for h in self.half]

    def tile(self, panel_low, a, s):
        return 2 * (2 * panel_low + a) + s

    def sends(self, n):
        k = self.k
        s, a = n // 2, n % 2
        low = where(self.apart & (self.half[0] != self.row), self.low[1], self.low[0])
        first = self.low[0] == k
        source = [
            where(first, self.tile(1 - k, 0, 0), self.tile(1 - k, 0, 1)),
            where(first, self.tile(1 - k, 0, 1), self.tile(1 - k, 1, 1)),
            self.tile(k, 0, 0),
            self.tile(k, 1, 0),
        ][n]
        both = where(self.in_row[0], self.tile(1 - k, a, s), 2 * (2 * k + s) + a)
        both = where(self.in_row[0] & self.in_col[0], source, both)
        return where(self.together, both, self.tile(low, a, s))

    def message(self, over_row, k):
        first = k == 0 if over_row else k != 0
        return where(k == self.k, where(first, FIRST, SECOND), where(first, FIRST_SIB, SECOND_SIB))

    def passed(self, k):
        return where(k == self.k, PASSED, PASSED_SIB)

    def square(self, base, i, j):
        if i == j:
            return base, jnp.int32(UPPER if i else LOWER)
        return base + 1, jnp.int32(PLAIN if i else TURNED)

    def diagonal(self, over_row, p, i, j):
        return self.square(self.message(over_row, self.low[p]) + 2, i, j)

    def mixed(self, over_row, i, j):
        return self.message(over_row, self.low[i]) + j, jnp.int32(i)

    def pick(self, cond, a, b):
        return where(cond, a[0], b[0]), where(cond, a[1], b[1])

    def rows(self, p, t, s, a):
        here = where(self.q[p] == self.col, OWN, SIB) + 2 * (2 * t + s) + a, jnp.int32(0)
        plain = self.message(False, jnp.int32(t)) + 2 * s + a, jnp.int32(1)
        own = self.square(self.message(False, jnp.int32(t)), s, a)
        plain = self.pick(self.equal & (self.low[p] == t), own, plain)
        same = self.diagonal(False, p, s, a)
        if p == 0:
            cross = self.mixed(False, s, a)
        else:
            cross = self.mixed(False, a, s)
            cross = cross[0], 1 - cross[1]
        both = self.pick(self.low[p] == t, same, cross)
        beside = self.pick(self.together, both, plain)
        passed = self.message(True, jnp.int32(t)) + 2 * s + a, jnp.int32(1)
        kept = self.message(False, jnp.int32(t)) + 2 * s + a, jnp.int32(0)
        far = self.pick(self.together & (self.low[p] == t), kept, passed)
        return self.pick(self.in_col[p], here, self.pick(self.in_row[p], beside, far))

    def cols(self, p, a, s):
        here = self.tile(self.low[p], a, s), jnp.int32(0)
        plain = self.message(True, self.k) + 2 * s + a, jnp.int32(0)
        own = self.square(self.message(True, self.k), a, s)
        plain = self.pick(self.equal & self.in_col[p] & (self.low[p] == self.k), own, plain)
        kept = self.message(False, self.k) + 2 * s + a, jnp.int32(1)
        passed = self.pick(self.low[p] == self.k, kept, plain)
        same = self.diagonal(True, p, a, s)
        if p == 0:
            cross = self.mixed(True, s, a)
            cross = cross[0], 1 - cross[1]
        else:
            cross = self.mixed(True, a, s)
        source = self.pick(self.low[p] == self.k, same, cross)
        both = self.pick(self.in_col[p], source, passed)
        far = self.pick(self.together, both, plain)
        return self.pick(self.in_row[p], here, far)

    def cross(self, i, a):
        mine = self.pick(self.low[1] == 0, self.rows(0, 0, i, a), self.rows(0, 1, i, a))
        turned = self.pick(self.low[0] == 0, self.rows(1, 0, a, i), self.rows(1, 1, a, i))
        turned = turned[0], 1 - turned[1]
        equal_near = self.square(self.message(True, self.low[1]), i, a)
        near = self.pick(self.equal, equal_near, self.mixed(True, i, a))
        equal_far = self.square(self.passed(self.low[0]), i, a)
        both_far = self.passed(self.low[i]) + a, jnp.int32(i)
        far = self.pick(self.equal, equal_far, both_far)
        outside = self.pick(self.in_col[1], near, far)
        return self.pick(self.in_row[1], mine, self.pick(self.in_row[0], turned, outside))


def quarter_of(tile, number, size):
    down = pl.multiple_of(lax.div(number, 2) * size, size)
    along = pl.multiple_of(lax.rem(number, 2) * size, size)
    return tile[pl.ds(down, size), pl.ds(along, size)]


def tie_kernel(_, __, ___):
    pass


TOKEN = jax.ShapeDtypeStruct((8, 128), F32)


def tie(x, *after, params=PARAMS):
    for other in after:
        x = pl.pallas_call(
            tie_kernel,
            out_shape=jax.ShapeDtypeStruct(x.shape, x.dtype),
            in_specs=[ANY, ANY],
            out_specs=ANY,
            input_output_aliases={0: 0},
            compiler_params=params,
        )(x, other)
    return x


def first_kernel(index_far, working, obs_far, rotation_far, order_far, message, own, *rest):
    sent, (index, tile, obs, rotation, order, moved, sems) = rest[:-7], rest[-7:]
    pairs = (
        (order_far, order),
        (rotation_far, rotation),
        (obs_far, obs),
        (index_far, index),
        (working, tile),
    )
    copies = [pltpu.make_async_copy(far, near, sems.at[n]) for n, (far, near) in enumerate(pairs)]
    for copy in copies:
        copy.start()
    row, latent = lax.axis_index("row"), lax.axis_index("latent")
    times, own_vars, stations = obs.shape
    latents, all_vars = rotation.shape
    copies[0].wait()
    local = order[...] - row * stations
    spread = lax.broadcasted_iota(jnp.int32, (stations, stations), 0) == local
    spread = spread.astype(F32).astype(BF16)
    copies[1].wait()
    shape = (latents * times, times * own_vars)
    left = lax.broadcasted_iota(jnp.int32, shape, 0)
    right = lax.broadcasted_iota(jnp.int32, shape, 1)
    keep = lax.rem(left, times) == lax.div(right, own_vars)
    sel_l = lax.broadcasted_iota(jnp.int32, (latents * times, latents), 0)
    sel_l = lax.div(sel_l, times) == lax.broadcasted_iota(jnp.int32, (latents * times, latents), 1)
    pick_v = lax.broadcasted_iota(jnp.int32, (all_vars, times * own_vars), 1)
    pick_v = lax.rem(pick_v, own_vars) + latent * own_vars
    pick_v = pick_v == lax.broadcasted_iota(jnp.int32, (all_vars, times * own_vars), 0)
    sel_l = sel_l.astype(F32).astype(BF16)
    pick_v = pick_v.astype(F32).astype(BF16)
    lefts = []
    for piece in pieces(rotation[...], 3):
        wide = dot(sel_l, piece, 1, 0).astype(BF16)
        wide = dot(wide, pick_v, 1, 0)
        lefts.append(jnp.where(keep, wide, 0.0).astype(BF16))
    copies[2].wait()
    flat = obs[...].reshape(times * own_vars, stations)
    total = sum(dot(wide, flat, 1, 0) for wide in lefts)
    moved[...] = dot(total.astype(BF16), spread, 1, 0).reshape(moved.shape)
    own[...] = moved[latent]
    for shift, out in enumerate(sent, 1):
        out[...] = moved[lax.rem(latent + shift, latents)].astype(BF16)
    copies[3].wait()
    here = Place(index)
    copies[4].wait()
    size = message.shape[1]
    starts = [0, size, 2 * size + ROWS, 3 * size + ROWS]
    for n, start in enumerate(starts):
        message[pl.ds(start, size)] = quarter_of(tile, here.sends(n), size)
    upper = quarter_of(tile, here.tile(here.k, 1, 1), size).astype(F32)
    down = lax.broadcasted_iota(jnp.int32, (size, size), 0)
    along = lax.broadcasted_iota(jnp.int32, (size, size), 1)
    triangles = jnp.where(down >= along, quarter_of(tile, here.tile(here.k, 0, 0), size).astype(F32), upper).astype(BF16)
    middle = jnp.sum(jnp.where(down == along, upper, 0.0), axis=0, keepdims=True)
    message[pl.ds(2 * size, ROWS)] = jnp.broadcast_to(middle, (ROWS, size)).astype(BF16)
    source = here.in_row[0] & here.in_col[0]

    @pl.when(source & here.equal & (here.low[0] == here.k))
    def _():
        message[pl.ds(starts[0], size)] = triangles

    @pl.when(source & here.together)
    def _():
        message[pl.ds(starts[2], size)] = triangles


def field_kernel(index, own, *rest):
    got, (field, rhs) = rest[:-2], rest[-2:]
    total = own[...]
    for part in got:
        total = total + part[...].astype(F32)
    field[...] = total
    width = rhs.shape[2]
    for p in range(rhs.shape[0]):
        inside = pl.ds(pl.multiple_of(lax.rem(index[p], 2) * width, width), width)
        rhs[p] = field[:, inside].astype(BF16)


def entries_of(here):
    entries = []
    for p in range(2):
        entries += [here.rows(p, n // 4, n // 2 % 2, n % 2) for n in range(8)]
    for p in range(2):
        entries += [here.cols(p, n // 2, n % 2) for n in range(4)]
    return entries + [here.cross(n // 2, n % 2) for n in range(4)]


def is_late(slot):
    return slot >= SECOND


def assemble(blocks, pool, middles, table, flip, base, wanted, earlier=None):
    size = pool.shape[1]

    def step(n, _):
        down = pl.ds(pl.multiple_of(n * size, size), size)
        for side in range(2):
            slot = table[2 * n + side]
            turn = flip[2 * n + side]
            along = pl.ds(side * size, size)
            here = wanted(slot)

            if earlier is not None:

                @pl.when(jnp.logical_not(here))
                def _():
                    blocks[down, along] = earlier[down, along]

            @pl.when(here & (turn == PLAIN))
            def _():
                blocks[down, along] = pool[slot - base]

            @pl.when(here & (turn == TURNED))
            def _():
                blocks[down, along] = pool[slot - base].T

            @pl.when(here & (turn >= LOWER))
            def _():
                both = pool[slot - base].astype(F32)
                i = lax.broadcasted_iota(jnp.int32, (size, size), 0)
                j = lax.broadcasted_iota(jnp.int32, (size, size), 1)
                lower = jnp.where(i >= j, both, both.T)
                middle = middles[lax.div(slot - base, 4)].astype(F32)[0:1]
                upper = jnp.where(i == j, middle, jnp.where(i < j, both, both.T))
                blocks[down, along] = jnp.where(turn == LOWER, lower, upper).astype(BF16)

        return 0

    lax.fori_loop(0, blocks.shape[0] // size, step, 0)


def unpack(ref, pool, middles, slot, number):
    size = pool.shape[1]
    pool[slot] = ref[pl.ds(0, size)]
    pool[slot + 1] = ref[pl.ds(size, size)]
    middles[number] = ref[pl.ds(2 * size, ROWS)]
    if ref.shape[0] > 3 * size:
        pool[slot + 2] = ref[pl.ds(2 * size + ROWS, size)]
        pool[slot + 3] = ref[pl.ds(3 * size + ROWS, size)]


def early_kernel(index, working, sibling, first, first_sib, blocks, table, flip, pool, middles):
    here = Place(index)
    size = pool.shape[1]
    for n, (slot, turn) in enumerate(entries_of(here)):
        table[n] = slot
        flip[n] = turn

    def tiles(n, _):
        down = pl.ds(pl.multiple_of(n * size, size), size)
        for side in range(2):
            along = pl.ds(side * size, size)
            pool[OWN + 2 * n + side] = working[down, along]
            pool[SIB + 2 * n + side] = sibling[down, along]
        return 0

    lax.fori_loop(0, working.shape[0] // size, tiles, 0)
    unpack(first, pool, middles, FIRST, FIRST // 4)
    unpack(first_sib, pool, middles, FIRST_SIB, FIRST_SIB // 4)
    assemble(blocks, pool, middles, table, flip, 0, lambda slot: jnp.logical_not(is_late(slot)))


def factor_kernel(
    index, table, flip, working, earlier, second, second_sib, passed, passed_sib,
    inverse, field, rhs_far, trailing, panels, whitened,
    blocks, pool, middles, factors0, factors1, turned0, turned1, rhs_near, result, sems,
):
    here = Place(index)
    size = pool.shape[1]
    tall, wide = working.shape
    width = inverse.shape[1]
    share = panels.shape[2]

    for n, ref in enumerate((second, second_sib, passed, passed_sib)):
        unpack(ref, pool, middles, 4 * n, n)
    assemble(blocks, pool, middles, table, flip, SECOND, is_late, earlier)

    rows0, rows1 = pl.ds(0, tall), pl.ds(tall, tall)
    cols0, cols1 = pl.ds(2 * tall, width), pl.ds(2 * tall + width, width)
    cross = pl.ds(2 * tall + 2 * width, width)
    inv0, inv1 = inverse[0], inverse[1]

    by_lower(blocks[cross], inv0, factors0, slice(tall, tall + width))
    lower_by(inv0, blocks[cols0], turned0)
    by_lower(blocks[rows0], inv0, factors0, slice(0, tall))
    mixed = factors0[pl.ds(tall, width)]

    got = blocks[cols1].astype(F32) - dot(mixed, turned0[...], 1, 0)
    lower_by(inv1, got.astype(BF16), turned1)
    got = blocks[rows1].astype(F32) - dot(factors0[rows0], mixed, 1, 1)
    by_lower(got.astype(BF16), inv1, factors1, slice(0, tall))

    lanes = pl.ds(pl.multiple_of(here.col * share, share), share)
    copies = [
        pltpu.make_async_copy(factors0.at[rows0, lanes], panels.at[0], sems.at[0]),
        pltpu.make_async_copy(factors1.at[:, lanes], panels.at[1], sems.at[1]),
    ]
    copies[0].start()
    copies[1].start()
    parts = sems.shape[0] - 2
    for n in range(parts):
        down = pl.ds(n * tall // parts, tall // parts)
        change = dot(factors0[down], turned0[...], 1, 0) + dot(factors1[down], turned1[...], 1, 0)
        result[down] = working[down].astype(F32) - change
        copies.append(pltpu.make_async_copy(result.at[down], trailing.at[down], sems.at[2 + n]))
        copies[-1].start()

    for p in range(2):
        inside = pl.ds(pl.multiple_of(here.low[p] * width, width), width)

        @pl.when(here.in_row[p])
        def _():
            rhs_near[p] = field[:, inside]

        @pl.when(jnp.logical_not(here.in_row[p]))
        def _():
            rhs_near[p] = rhs_far[p].astype(F32)

    def solve(rhs, inv):
        return sum(dot(piece, inv, 1, 1) for piece in pieces(rhs, 2)).astype(BF16)

    solved0 = solve(rhs_near[0], inv0)
    solved1 = solve(rhs_near[1] - dot(solved0, mixed, 1, 1), inv1)
    whitened[...] = field[...] - dot(solved0, factors0[rows0], 1, 1) - dot(solved1, factors1[...], 1, 1)
    for copy in copies:
        copy.wait()


def local(observations, rotation, ordering, working, factor_inverse, panel_index):
    latents = rotation.shape[1]
    latent_count = lax.axis_size("latent")
    times, own_vars, stations = observations.shape
    matrix = working[0]
    inverse = factor_inverse[0]
    tall, wide = matrix.shape
    panel_count, width, _ = inverse.shape
    size = width // 2
    share = width // lax.axis_size("col")

    cols = lax.axis_size("col")

    def across_rows(x):
        return lax.ppermute(x, "row", [(0, 1), (1, 0)])

    def siblings(x):
        return lax.ppermute(x, "col", [(i, i ^ 1) for i in range(cols)])

    def neighbours(x, row_first):
        pairs = []
        for i in range(2):
            for j in range(cols):
                over_row = (j % 2 == 0) == row_first
                to = (1 - i, j) if over_row else (i, j ^ 2)
                pairs.append((i * cols + j, to[0] * cols + to[1]))
        return lax.ppermute(x, ("row", "col"), pairs)

    message = jax.ShapeDtypeStruct((4 * size + ROWS, size), BF16)
    sibling = siblings(matrix)
    sent_message, own, *sent = pl.pallas_call(
        first_kernel,
        out_shape=[message, jax.ShapeDtypeStruct((times, stations), F32)]
        + [jax.ShapeDtypeStruct((times, stations), BF16)] * (latent_count - 1),
        in_specs=[ANY] * 5,
        out_specs=[VMEM] * (1 + latent_count),
        scratch_shapes=[
            pltpu.SMEM(panel_index.shape, jnp.int32),
            pltpu.VMEM(matrix.shape, BF16),
            pltpu.VMEM(observations.shape, BF16),
            pltpu.VMEM(rotation.shape[::-1], F32),
            pltpu.VMEM((1, stations), jnp.int32),
            pltpu.VMEM((latents, times, stations), F32),
            pltpu.SemaphoreType.DMA((5,)),
        ],
        compiler_params=WIDE,
    )(panel_index, matrix, observations, rotation.T, ordering[None])
    first = neighbours(sent_message, True)
    got = []
    for shift, part in enumerate(sent, 1):
        pairs = [(i, (i + shift) % latent_count) for i in range(latent_count)]
        got.append(lax.ppermute(part, "latent", pairs))

    second = neighbours(sent_message, False)
    first = tie(first, got[0], own, *got[1:])
    field, rhs = pl.pallas_call(
        field_kernel,
        out_shape=(
            jax.ShapeDtypeStruct((times, stations), F32),
            jax.ShapeDtypeStruct((panel_count, times, width), BF16),
        ),
        in_specs=[SMEM] + [VMEM] * latent_count,
        out_specs=(VMEM, VMEM),
        compiler_params=PARAMS,
    )(panel_index, own, *got)
    rhs_far = across_rows(rhs)
    first_sib = siblings(first)
    passed = neighbours(first[: 2 * size + ROWS], False)
    block_shape = jax.ShapeDtypeStruct((14 * size, width), BF16)
    table_shape = jax.ShapeDtypeStruct((28,), jnp.int32)
    blocks, table, flip = pl.pallas_call(
        early_kernel,
        out_shape=(block_shape, table_shape, table_shape),
        in_specs=[SMEM] + [VMEM] * 4,
        out_specs=(VMEM, SMEM, SMEM),
        scratch_shapes=[
            pltpu.VMEM((SECOND, size, size), BF16),
            pltpu.VMEM((SECOND // 4, ROWS, size), BF16),
        ],
        compiler_params=PARAMS,
    )(panel_index, matrix, sibling, first, first_sib)

    second = tie(second, rhs_far, table)
    second_sib, passed_sib = siblings(second), siblings(passed)

    trailing, panels, whitened = pl.pallas_call(
        factor_kernel,
        out_shape=(
            jax.ShapeDtypeStruct((tall, wide), F32),
            jax.ShapeDtypeStruct((panel_count, tall, share), BF16),
            jax.ShapeDtypeStruct((times, stations), F32),
        ),
        in_specs=[SMEM] * 3 + [VMEM] * 9,
        out_specs=(HBM, HBM, VMEM),
        scratch_shapes=[
            pltpu.VMEM(block_shape.shape, BF16),
            pltpu.VMEM((POOL - SECOND, size, size), BF16),
            pltpu.VMEM(((POOL - SECOND) // 4, ROWS, size), BF16),
            pltpu.VMEM((tall + width, width), BF16),
            pltpu.VMEM((tall, width), BF16),
            pltpu.VMEM((width, wide), BF16),
            pltpu.VMEM((width, wide), BF16),
            pltpu.VMEM((panel_count, times, width), F32),
            pltpu.VMEM((tall, wide), F32),
            pltpu.SemaphoreType.DMA((6,)),
        ],
        compiler_params=PARAMS,
    )(
        panel_index, table, flip, matrix, blocks, second, second_sib, passed, passed_sib,
        inverse, field, rhs_far,
    )
    return trailing[None], panels[None], whitened[None]


def solution(mesh):
    return jax.shard_map(
        local,
        mesh=mesh,
        in_specs=(
            P("col", "latent", "row"),
            P(),
            P("row"),
            P("latent", "row", "col"),
            P("latent", None, None, None),
            P(),
        ),
        out_specs=(
            P("latent", "row", "col"),
            P("latent", None, "row", "col"),
            P("latent", "col", "row"),
        ),
        check_vma=False,
    )
```
